32 devices in a mesh: hst: 8 (over z, y), local: 4 (over x, core).
Axes of the slice: x: 2, y: 2, z: 4, core: 2. Of those that a mesh axis runs over, the one named last changes fastest.
Arguments:
- embedding: float32 [65536, 256], P(('hst', 'local')), may hold values from -6 to 6
- row_accum: float32 [65536], P(('hst', 'local')), may hold values from 0.5 to 8
- lookup_grads: bfloat16 [65536, 256], P(('hst', 'local')), may hold values from -3 to 3
- lookup_slot: int32 [65536], P(('hst', 'local')), may hold values from 0 to 1023, as said below
- owner_rows: int32 [32, 8, 32], P(('hst', 'local')), may hold values from -1 to 2047, as said below
Outputs:
- new_embedding: float32 [65536, 256], P(('hst', 'local'))
- new_accum: float32 [65536], P(('hst', 'local'))
- fresh_rows: bfloat16 [65536, 256], P(('hst', 'local'))
The draws below stay inside these ranges and needn't reach their ends.
Inputs may be any that keep to these rules, and one draw needn't show every extreme that they name: For a lookup of host s, lookup_slot = o * 32 + c with owner device o and c below that host's count of live slots for o; owners with low numbers are looked up far more often. owner_rows[o, s, c] is live (not -1) exactly for c below a count of 1 to 32; every (o, s) with o mod 8 equal to s has 32 live slots; live rows of one (o, s) are distinct; a few leading slots name the same row for every host s.
All inputs are finite; a program needn't handle non-finite values.
Results may differ from the reference program's by a relative error of at most 0.0039.
Values may be sent and summed in bfloat16 or wider, within the bound.
No kernel may reach another device: no remote copies, remote signals or barrier semaphores. Data moves between devices by JAX's collectives and lax.ppermute only.
A program may use at most 64 MiB of HBM per device.

```python
import math
import jax
import jax.numpy as jnp
from jax import lax

E = 256
ROWS_DEV = 2048
TOK_DEV = 2048
CAP = 32
OWNERS = 32
TOKENS = 65536
TABLE_ROWS = 65536
N_HST = 8
N_LOCAL = 4


def bucket_counts(key):
    key = jax.random.fold_in(key, 100)
    counts = jax.random.randint(key, (N_HST, OWNERS), 1, CAP + 1)
    is_full = jnp.arange(OWNERS)[None, :] % N_HST == jnp.arange(N_HST)[:, None]
    return jnp.where(is_full, CAP, counts).astype(jnp.int32)


def draw_lookup_slot(key, part):
    counts = bucket_counts(key)
    key = jax.random.fold_in(key, 1)
    key_a, key_b, key_c, key_d = jax.random.split(key, 4)
    pick_a = jax.random.randint(key_a, (TOKENS,), 0, OWNERS)
    pick_b = jax.random.randint(key_b, (TOKENS,), 0, OWNERS)
    pick_c = jax.random.randint(key_c, (TOKENS,), 0, OWNERS)
    owner_pick = jnp.minimum(pick_a, jnp.minimum(pick_b, pick_c))
    host_of = jnp.arange(TOKENS) // (TOK_DEV * N_LOCAL)
    host_count = counts[host_of, owner_pick]
    position = jax.random.randint(key_d, (TOKENS,), 0, CAP) % host_count
    slots = owner_pick * CAP + position
    token_pos = jnp.arange(TOKENS)
    slots = jnp.where(token_pos == TOKENS - 1, OWNERS * CAP - 1, slots)
    slots = jnp.where(token_pos == 0, 0, slots)
    return slots.astype(jnp.int32)


def draw_owner_rows(key, part):
    counts = bucket_counts(key)
    key = jax.random.fold_in(key, 2)
    key_a, key_b = jax.random.split(key, 2)
    span_rows = ROWS_DEV // CAP
    base_pick = jax.random.randint(key_a, (OWNERS, N_HST, CAP), 0, span_rows)
    shared = jax.random.randint(key_b, (OWNERS, 1, CAP), 0, span_rows)
    slot_pos = jnp.arange(CAP)[None, None, :]
    is_hot = slot_pos < max(1, CAP // 4)
    corner = (jnp.arange(OWNERS)[:, None, None] == 0) & (jnp.arange(N_HST)[None, :, None] == 0) & (slot_pos == CAP - 1)
    base_pick = jnp.where(corner, span_rows - 1, base_pick)
    local_row = slot_pos * span_rows + jnp.where(is_hot, shared, base_pick)
    is_live = slot_pos < counts.T[:, :, None]
    return jnp.where(is_live, local_row, -1).astype(jnp.int32)


def levels(key, extent, cuts, smallest, largest):
    def one(dim, parts):
        steps = jax.random.uniform(jax.random.fold_in(jax.random.fold_in(key, 6), dim), (parts,), jnp.float32, smallest / len(cuts), largest / len(cuts))
        return jnp.repeat(jnp.exp(steps), extent[dim] // parts).reshape((-1,) + (1,) * (len(extent) - dim - 1))

    loudness = one(*cuts[0])
    for cut in cuts[1:]:
        loudness = loudness * one(*cut)
    return loudness


def normal_values(stream_key, shape, width, limit, cuts=(), kind=jnp.bfloat16):
    level = levels(stream_key, shape, cuts, -0.22, 0.18) if cuts else 1.0
    result = jax.random.normal(stream_key, shape, jnp.float32) * width * level
    return jnp.minimum(jnp.maximum(result, -limit), limit).astype(kind)


def setup_inputs(seed: int = 0) -> dict:
    keys = jax.random.split(jax.random.key(seed), 6)
    return {
        "embedding": normal_values(keys[0], (TABLE_ROWS, E), 1.0, 6.0, ((0, 32),), jnp.float32),
        "row_accum": jnp.clip(jnp.exp(math.log(8.0) - 2.7725887 * jax.random.uniform(keys[1], (TABLE_ROWS,), jnp.float32) ** levels(keys[1], (TABLE_ROWS,), ((0, 32),), -0.2, 0.2)), 0.5, 8.0),
        "lookup_grads": normal_values(keys[2], (TOKENS, E), 0.5, 3.0, ((0, 32),)),
        "lookup_slot": draw_lookup_slot(jax.random.fold_in(keys[5], 71), 0),
        "owner_rows": draw_owner_rows(jax.random.fold_in(keys[5], 71), 0),
    }


def reference(embedding, row_accum, lookup_grads, lookup_slot, owner_rows):
    n_owner = N_HST * N_LOCAL
    slot_total = n_owner * CAP
    grad_blocks = lookup_grads.reshape(n_owner, TOK_DEV, E)
    slot_blocks = lookup_slot.reshape(n_owner, TOK_DEV)

    def add_device(carry, device):
        grad_part = lax.dynamic_index_in_dim(grad_blocks, device, 0, keepdims=False)
        slot_part = lax.dynamic_index_in_dim(slot_blocks, device, 0, keepdims=False)
        partial_value = jax.ops.segment_sum(grad_part.astype(jnp.float32), slot_part, num_segments=slot_total)
        partial_value = lax.optimization_barrier(partial_value.astype(jnp.bfloat16)).astype(jnp.float32)
        host_of = device // N_LOCAL
        return (carry.at[host_of].add(partial_value), None)
    start = jnp.zeros((N_HST, slot_total, E), jnp.float32)
    slot_grad, _ = lax.scan(add_device, start, jnp.arange(n_owner, dtype=jnp.int32))
    slot_grad = lax.optimization_barrier(slot_grad.astype(jnp.bfloat16)).astype(jnp.float32)
    grid = slot_grad.reshape(N_HST, n_owner, CAP, E).transpose(1, 0, 2, 3).reshape(-1, E)
    owner_base = (jnp.arange(n_owner, dtype=jnp.int32) * ROWS_DEV)[:, None, None]
    is_live = owner_rows >= 0
    target = jnp.where(is_live, owner_rows + owner_base, TABLE_ROWS).astype(jnp.int32)
    row_grad = jax.ops.segment_sum(grid, target.reshape(-1), num_segments=TABLE_ROWS + 1)[:TABLE_ROWS]
    new_accum = row_accum + lax.optimization_barrier(jnp.mean(row_grad * row_grad, axis=1))
    new_embedding = embedding - 0.1 * row_grad / jnp.sqrt(new_accum)[:, None]
    safe_rows = jnp.where(is_live, target, 0).astype(jnp.int32)
    picked = jnp.take(new_embedding, safe_rows.reshape(-1), axis=0).reshape(n_owner, N_HST, CAP, E)
    picked = jnp.where(is_live[:, :, :, None], picked, 0.0).astype(jnp.bfloat16)
    host_cache = picked.transpose(1, 0, 2, 3).reshape(N_HST * slot_total, E)
    host_of = jnp.arange(TOKENS, dtype=jnp.int32) // (TOK_DEV * N_LOCAL)
    fresh_rows = jnp.take(host_cache, host_of * slot_total + lookup_slot, axis=0)
    return (new_embedding, new_accum, fresh_rows)
```

```python
import functools

import jax
import jax.numpy as jnp
from jax import lax
from jax.experimental import pallas as pl
from jax.experimental.pallas import tpu as pltpu
from jax.sharding import Mesh, PartitionSpec as P

MIB = 1024 * 1024


def bits_of(n):
    bits = n.bit_length() - 1
    assert n == 1 << bits
    return bits


def planes(n_hst):
    return 1 << (bits_of(n_hst) // 2)


def z_place(z, n_z, back):
    return (z - n_z // 2 if back else n_z // 2 - z) & (n_z - 1)


def member(host, chip, n_hst, chips, back):
    n_y = planes(n_hst)
    n_z = n_hst // n_y
    z, y = host // n_y, host % n_y
    return (y * chips + chip) * n_z + z_place(z, n_z, back)


def slot_place(ids, capacity, half, back):
    n_hst, chips = lax.axis_size("hst"), lax.axis_size("x")
    n_y = planes(n_hst)
    n_z = n_hst // n_y
    cap_bits, z_bits, yx_bits = bits_of(capacity), bits_of(n_z), bits_of(n_y * chips)
    other = ((ids >> cap_bits) & 1) ^ lax.axis_index("core")
    z = z_place(ids >> (cap_bits + 1 + yx_bits), n_z, back)
    yx = (ids >> (cap_bits + 1)) & ((1 << yx_bits) - 1)
    return other * half + (((yx << z_bits) + z) << cap_bits) + (ids & (capacity - 1))


def column(row):
    return jnp.transpose(jnp.broadcast_to(row, (128, 128)))


def matches(a, b):
    return jnp.where(a == b, jnp.bfloat16(1), jnp.bfloat16(0))


def small(a):
    return a.astype(jnp.int16)


def onehot_lines(place, block):
    shape = (16, place.shape[1])
    slot = small(lax.broadcasted_iota(jnp.int32, shape, 0))
    place = small(jnp.broadcast_to(place, shape))
    return jnp.concatenate(
        [matches(slot, place - jnp.int16(start)) for start in range(0, block, 16)], axis=0
    )


def load_kernel(grads_ref, out_ref, sems):
    chunks = sems.shape[0]
    piece = out_ref.shape[0] // chunks
    copies = []
    for chunk in range(chunks):
        at = pl.ds(chunk * piece, piece)
        copies.append(pltpu.make_async_copy(grads_ref.at[at], out_ref.at[at], sems.at[chunk]))
        copies[-1].start()
    for copy in copies:
        copy.wait()


def load(grads):
    return pl.pallas_call(
        load_kernel,
        in_specs=[pl.BlockSpec(memory_space=pl.ANY)],
        out_specs=pl.BlockSpec(memory_space=pltpu.VMEM),
        out_shape=jax.ShapeDtypeStruct(grads.shape, grads.dtype),
        scratch_shapes=[pltpu.SemaphoreType.DMA((16,))],
        compiler_params=pltpu.CompilerParams(vmem_limit_bytes=52 * MIB),
        cost_estimate=pl.CostEstimate(
            flops=0, bytes_accessed=4 * grads.shape[0] * grads.shape[1], transcendentals=0
        ),
        name="load",
    )(grads)


def sums_kernel(ids_ref, grads_ref, out_ref, *, base, half, capacity):
    block = out_ref.shape[0]
    place = slot_place(ids_ref[...], capacity, half, False) - (base + pl.program_id(0) * block)
    out_ref[...] = jnp.dot(
        onehot_lines(place, block), grads_ref[...], preferred_element_type=jnp.float32
    ).astype(out_ref.dtype)


def slot_sums(ids, grads, base, half, capacity):
    tokens, width = grads.shape
    block = min(512, half)
    return pl.pallas_call(
        functools.partial(sums_kernel, base=base, half=half, capacity=capacity),
        grid=(half // block,),
        in_specs=[
            pl.BlockSpec((1, tokens), lambda i: (0, 0)),
            pl.BlockSpec((tokens, width), lambda i: (0, 0)),
        ],
        out_specs=pl.BlockSpec((block, width), lambda i: (i, 0)),
        out_shape=jax.ShapeDtypeStruct((half, width), jnp.bfloat16),
        compiler_params=pltpu.CompilerParams(vmem_limit_bytes=16 * MIB),
        cost_estimate=pl.CostEstimate(
            flops=2 * half * tokens * width,
            bytes_accessed=2 * (tokens + half) * width,
            transcendentals=0,
        ),
        name="slot_sums",
    )(ids, grads)


def add_kernel(a_ref, b_ref, out_ref, lines, sems):
    chunks = sems.shape[0]
    piece = lines.shape[0] // chunks
    copies = []
    for chunk in range(chunks):
        at = slice(chunk * piece, (chunk + 1) * piece)
        total = a_ref[at, :].astype(jnp.float32) + b_ref[at, :].astype(jnp.float32)
        lines[at, :] = total.astype(jnp.bfloat16)
        window = pl.ds(chunk * piece, piece)
        copies.append(
            pltpu.make_async_copy(lines.at[window], out_ref.at[window], sems.at[chunk])
        )
        copies[-1].start()
    for copy in copies:
        copy.wait()


def add(a, b):
    vmem = pl.BlockSpec(memory_space=pltpu.VMEM)
    return pl.pallas_call(
        add_kernel,
        in_specs=[vmem] * 2,
        out_specs=pl.BlockSpec(memory_space=pl.ANY),
        out_shape=jax.ShapeDtypeStruct(a.shape, a.dtype),
        scratch_shapes=[pltpu.VMEM(a.shape, a.dtype), pltpu.SemaphoreType.DMA((4,))],
        compiler_params=pltpu.CompilerParams(vmem_limit_bytes=24 * MIB),
        cost_estimate=pl.CostEstimate(
            flops=a.size, bytes_accessed=6 * a.size, transcendentals=0
        ),
        name="add",
    )(a, b)


def prepare_kernel(
    rows_ref, emb_ref, acc_ref, ids_ref, old_ref, old_acc_ref, same_ref, cols_ref, *, half, capacity
):
    place = slot_place(ids_ref[...], capacity, half, True)
    for start in range(0, cols_ref.shape[0], 128):
        cols_ref[start : start + 128, :] = small(column(place[:, start : start + 128]))
    slots = rows_ref.shape[1]
    rows_dev = emb_ref.shape[0]
    rows = rows_ref[...]
    high = emb_ref[...].astype(jnp.bfloat16)
    low = (emb_ref[...] - high.astype(jnp.float32)).astype(jnp.bfloat16)
    row_lane = lax.broadcasted_iota(jnp.int32, (128, 128), 1)
    for start in range(0, slots, 128):
        at = slice(start, start + 128)
        col = column(rows[:, at])
        tiles = []
        acc = jnp.zeros((128, 128), jnp.float32)
        for tile in range(rows_dev // 128):
            hit = (row_lane + tile * 128) == col
            tiles.append(jnp.where(hit, 1.0, 0.0).astype(jnp.bfloat16))
            acc = acc + jnp.where(hit, acc_ref[tile : tile + 1, :], 0.0)
        onehot = jnp.concatenate(tiles, axis=1)
        old_ref[at, :] = jnp.dot(
            onehot, high, preferred_element_type=jnp.float32
        ) + jnp.dot(onehot, low, preferred_element_type=jnp.float32)
        acc = jnp.sum(acc, axis=1, keepdims=True)
        old_acc_ref[at, :] = jnp.where(col >= 0, acc, 1.0)
        for other in range(0, slots, 128):
            them = rows[:, other : other + 128]
            same_ref[at, other : other + 128] = jnp.where(
                (col == them) & (col >= 0), 1.0, 0.0
            ).astype(jnp.bfloat16)


def prepare(rows, embedding, row_accum, ids, half, capacity):
    rows_dev, width = embedding.shape
    slots = rows.shape[1]
    tokens = ids.shape[1]
    vmem = pl.BlockSpec(memory_space=pltpu.VMEM)
    return pl.pallas_call(
        functools.partial(prepare_kernel, half=half, capacity=capacity),
        in_specs=[vmem] * 4,
        out_specs=[vmem] * 4,
        out_shape=[
            jax.ShapeDtypeStruct((slots, width), jnp.float32),
            jax.ShapeDtypeStruct((slots, 128), jnp.float32),
            jax.ShapeDtypeStruct((slots, slots), jnp.bfloat16),
            jax.ShapeDtypeStruct((tokens, 128), jnp.int16),
        ],
        compiler_params=pltpu.CompilerParams(vmem_limit_bytes=24 * MIB),
        cost_estimate=pl.CostEstimate(
            flops=4 * rows_dev * slots * width,
            bytes_accessed=4 * rows_dev * width,
            transcendentals=0,
        ),
        name="prepare",
    )(rows, embedding, row_accum.reshape(rows_dev // 128, 128), ids)


def pick_kernel(arrived_ref, old_ref, acc_ref, same_ref, back_ref, sums_ref, lines, sems, *, places, back_places):
    capacity, width = arrived_ref.shape[1:]
    for host, members in enumerate(places):
        total = arrived_ref[members[0]].astype(jnp.float32)
        for place in members[1:]:
            total = total + arrived_ref[place].astype(jnp.float32)
        sums_ref[host * capacity : (host + 1) * capacity, :] = total.astype(jnp.bfloat16)
    grad = jnp.dot(same_ref[...], sums_ref[...], preferred_element_type=jnp.float32)
    square = jnp.mean(grad * grad, axis=1, keepdims=True)
    rate = 0.1 * lax.rsqrt(acc_ref[...] + square)
    for side in range(0, width, 128):
        lanes = slice(side, side + 128)
        new = (old_ref[:, lanes] - rate * grad[:, lanes]).astype(jnp.bfloat16)
        for host, members in enumerate(back_places):
            for place in members:
                lines[place, :, lanes] = new[host * capacity : (host + 1) * capacity]
    cut = lines.shape[0] // sems.shape[0]
    copies = []
    for part in range(sems.shape[0]):
        at = pl.ds(part * cut, cut)
        copies.append(pltpu.make_async_copy(lines.at[at], back_ref.at[at], sems.at[part]))
        copies[-1].start()
    for copy in copies:
        copy.wait()


def pick(arrived, old, old_acc, same, places, back_places):
    _, capacity, width = arrived.shape
    slots = len(places) * capacity
    vmem = pl.BlockSpec(memory_space=pltpu.VMEM)
    return pl.pallas_call(
        functools.partial(pick_kernel, places=places, back_places=back_places),
        in_specs=[vmem] * 4,
        out_specs=[pl.BlockSpec(memory_space=pl.ANY), vmem],
        out_shape=[
            jax.ShapeDtypeStruct(arrived.shape, jnp.bfloat16),
            jax.ShapeDtypeStruct((slots, width), jnp.bfloat16),
        ],
        scratch_shapes=[
            pltpu.VMEM(arrived.shape, jnp.bfloat16),
            pltpu.SemaphoreType.DMA((2,)),
        ],
        compiler_params=pltpu.CompilerParams(vmem_limit_bytes=24 * MIB),
        cost_estimate=pl.CostEstimate(
            flops=2 * slots * slots * width,
            bytes_accessed=8 * slots * width,
            transcendentals=slots,
        ),
        name="pick",
    )(arrived, old, old_acc, same)


def update_kernel(rows_ref, sums_ref, emb_ref, acc_ref, new_emb_ref, new_acc_ref):
    block, width = emb_ref.shape
    onehot = onehot_lines(rows_ref[...] - pl.program_id(0) * block, block)
    grad = jnp.dot(onehot, sums_ref[...], preferred_element_type=jnp.float32)
    square = jnp.mean(grad * grad, axis=1, keepdims=True)
    diagonal = lax.broadcasted_iota(jnp.int32, (128, 128), 0) == lax.broadcasted_iota(
        jnp.int32, (128, 128), 1
    )
    for part in range(block // 128):
        at = slice(part * 128, part * 128 + 128)
        acc = column(acc_ref[0, part : part + 1, :]) + square[at]
        new_acc_ref[0, part : part + 1, :] = jnp.sum(
            jnp.where(diagonal, acc, 0.0), axis=0, keepdims=True
        )
        rate = 0.1 * lax.rsqrt(acc)
        for side in range(0, width, 128):
            lanes = slice(side, side + 128)
            new_emb_ref[at, lanes] = emb_ref[at, lanes] - rate * grad[at, lanes]


def update(rows, sums, embedding, row_accum):
    rows_dev, width = embedding.shape
    slots = rows.shape[1]
    block = 512
    steps = rows_dev // block
    accum = row_accum.reshape(steps, block // 128, 128)
    table = pl.BlockSpec((block, width), lambda i: (i, 0))
    line = pl.BlockSpec((1, block // 128, 128), lambda i: (i, 0, 0))
    new_emb, new_acc = pl.pallas_call(
        update_kernel,
        grid=(steps,),
        in_specs=[
            pl.BlockSpec((1, slots), lambda i: (0, 0)),
            pl.BlockSpec((slots, width), lambda i: (0, 0)),
            table,
            line,
        ],
        out_specs=[table, line],
        out_shape=[
            jax.ShapeDtypeStruct((rows_dev, width), jnp.float32),
            jax.ShapeDtypeStruct(accum.shape, jnp.float32),
        ],
        compiler_params=pltpu.CompilerParams(vmem_limit_bytes=16 * MIB),
        cost_estimate=pl.CostEstimate(
            flops=2 * rows_dev * slots * width,
            bytes_accessed=8 * rows_dev * width,
            transcendentals=rows_dev,
        ),
        name="update",
    )(rows, sums, embedding, accum)
    return new_emb, new_acc.reshape(rows_dev)


def chosen_rows(cols, cache, base):
    slots = cache.shape[0]
    lane = lax.broadcasted_iota(jnp.int32, cols.shape, 1)
    onehot = jnp.concatenate(
        [matches(cols, small(lane + (base + start))) for start in range(0, slots, 128)], axis=1
    )
    return jnp.dot(onehot, cache, preferred_element_type=jnp.float32)


def first_expand_kernel(cols_ref, cache_ref, out_ref):
    block = min(1024, MIB // cache_ref.shape[0])
    for start in range(0, out_ref.shape[0], block):
        at = slice(start, start + block)
        out_ref[at, :] = chosen_rows(cols_ref[at, :], cache_ref[...], 0).astype(jnp.bfloat16)


def second_expand_kernel(cols_ref, cache_ref, before_ref, out_ref, lines, sems):
    block = lines.shape[0] // sems.shape[0]
    copies = []
    for start in range(0, lines.shape[0], block):
        at = slice(start, start + block)
        rows = chosen_rows(cols_ref[at, :], cache_ref[...], cache_ref.shape[0])
        lines[at, :] = (rows + before_ref[at, :].astype(jnp.float32)).astype(jnp.bfloat16)
        window = pl.ds(start, block)
        copies.append(
            pltpu.make_async_copy(lines.at[window], out_ref.at[window], sems.at[start // block])
        )
        copies[-1].start()
    for copy in copies:
        copy.wait()


def expand(cols, cache, before=None):
    slots, width = cache.shape
    tokens = cols.shape[0]
    vmem = pl.BlockSpec(memory_space=pltpu.VMEM)
    last = before is not None
    return pl.pallas_call(
        second_expand_kernel if last else first_expand_kernel,
        in_specs=[vmem] * (2 + last),
        out_specs=pl.BlockSpec(memory_space=pltpu.HBM) if last else vmem,
        out_shape=jax.ShapeDtypeStruct((tokens, width), jnp.bfloat16),
        scratch_shapes=[
            pltpu.VMEM((tokens, width), jnp.bfloat16),
            pltpu.SemaphoreType.DMA((tokens // 256,)),
        ]
        if last
        else [],
        compiler_params=pltpu.CompilerParams(vmem_limit_bytes=32 * MIB),
        cost_estimate=pl.CostEstimate(
            flops=2 * slots * tokens * width,
            bytes_accessed=2 * (tokens + slots) * width,
            transcendentals=0,
        ),
        name="second_expand" if last else "first_expand",
    )(cols, cache, *([before] if last else []))


def local(embedding, row_accum, lookup_grads, lookup_slot, owner_rows):
    n_hst = lax.axis_size("hst")
    chips = lax.axis_size("x")
    width = embedding.shape[1]
    capacity = owner_rows.shape[2]
    half = n_hst * chips * capacity

    def swap(block):
        return lax.ppermute(block, "core", [(0, 1), (1, 0)])

    members = n_hst * chips

    def places(back):
        return [[member(h, x, n_hst, chips, back) for x in range(chips)] for h in range(n_hst)]

    def exchange(blocks, back):
        order = [0] * members
        for host, row in enumerate(places(back)):
            for chip, place in enumerate(row):
                order[place] = host * chips + chip
        blocks = blocks.reshape(members, capacity, width)
        return lax.all_to_all(
            blocks, ("hst", "x"), split_axis=0, concat_axis=0, axis_index_groups=[order], tiled=True
        )

    rows = owner_rows.reshape(1, n_hst * capacity)
    ids = lookup_slot.reshape(1, -1)
    grads = load(lookup_grads)
    arrived = swap(slot_sums(ids, grads, half, half, capacity))
    kept = slot_sums(ids, grads, 0, half, capacity)
    arrived = exchange(add(kept, arrived), False)
    old, old_acc, same, cols = prepare(rows, embedding, row_accum, ids, half, capacity)
    back, sums = pick(arrived, old, old_acc, same, places(False), places(True))
    cache = exchange(back, True).reshape(half, width)
    new_embedding, new_accum = update(rows, sums, embedding, row_accum)
    cache, new_embedding, new_accum = lax.optimization_barrier((cache, new_embedding, new_accum))

    other = swap(cache)
    fresh_rows = expand(cols, cache)
    fresh_rows = expand(cols, other, fresh_rows)
    return (new_embedding, new_accum, fresh_rows)


def solution(mesh):
    chips = mesh.shape["local"] // 2
    fine = Mesh(mesh.devices.reshape(mesh.shape["hst"], chips, 2), ("hst", "x", "core"))
    whole = ("hst", "x", "core")
    return jax.shard_map(
        local,
        mesh=fine,
        in_specs=(P(whole, None), P(whole), P(whole, None), P(whole), P(whole, None, None)),
        out_specs=(P(whole, None), P(whole), P(whole, None)),
        check_vma=False,
    )
```

```python
import functools

import jax
import jax.numpy as jnp
from jax import lax
from jax.experimental import pallas as pl
from jax.experimental.pallas import tpu as pltpu
from jax.sharding import Mesh, PartitionSpec as P

MIB = 1024 * 1024


def bits_of(n):
    bits = n.bit_length() - 1
    assert n == 1 << bits
    return bits


def planes(n_hst):
    return 1 << (bits_of(n_hst) // 2)


def chip_order(n_hst, chips, back):
    n_y = planes(n_hst)
    n_z, n_yx = n_hst // n_y, n_y * chips
    mid = n_z // 2
    if back:
        zs = [*range(mid, n_z), *reversed(range(mid))]
        return [z * n_yx + yx for z in zs for yx in reversed(range(n_yx))]
    zs = [*reversed(range(mid + 1)), *reversed(range(mid + 1, n_z))]
    return [z * n_yx + (at ^ (n_yx // 2)) for at in range(n_yx) for z in zs]


def slot_place(ids, capacity, half, back):
    cap_bits = bits_of(capacity)
    other = ((ids >> cap_bits) & 1) ^ lax.axis_index("core")
    chip = ids >> (cap_bits + 1)
    place = jnp.zeros_like(chip)
    for at, member in enumerate(chip_order(lax.axis_size("hst"), lax.axis_size("x"), back)):
        place = jnp.where(chip == member, at, place)
    return other * half + (place << cap_bits) + (ids & (capacity - 1))


def column(row):
    return jnp.transpose(jnp.broadcast_to(row, (128, 128)))


def matches(a, b):
    return jnp.where(a == b, jnp.bfloat16(1), jnp.bfloat16(0))


def small(a):
    return a.astype(jnp.int16)


def onehot_lines(place, block):
    shape = (16, place.shape[1])
    slot = small(lax.broadcasted_iota(jnp.int32, shape, 0))
    place = small(jnp.broadcast_to(place, shape))
    return jnp.concatenate(
        [matches(slot, place - jnp.int16(start)) for start in range(0, block, 16)], axis=0
    )


def load_kernel(grads_ref, out_ref, sems):
    chunks = sems.shape[0]
    piece = out_ref.shape[0] // chunks
    copies = []
    for chunk in range(chunks):
        at = pl.ds(chunk * piece, piece)
        copies.append(pltpu.make_async_copy(grads_ref.at[at], out_ref.at[at], sems.at[chunk]))
        copies[-1].start()
    for copy in copies:
        copy.wait()


def load(grads):
    return pl.pallas_call(
        load_kernel,
        in_specs=[pl.BlockSpec(memory_space=pl.ANY)],
        out_specs=pl.BlockSpec(memory_space=pltpu.VMEM),
        out_shape=jax.ShapeDtypeStruct(grads.shape, grads.dtype),
        scratch_shapes=[pltpu.SemaphoreType.DMA((2,))],
        compiler_params=pltpu.CompilerParams(vmem_limit_bytes=52 * MIB),
        cost_estimate=pl.CostEstimate(
            flops=0, bytes_accessed=4 * grads.shape[0] * grads.shape[1], transcendentals=0
        ),
        name="load",
    )(grads)


def sums_kernel(ids_ref, grads_ref, out_ref, *, base, half, capacity):
    block = out_ref.shape[0]
    place = slot_place(ids_ref[...], capacity, half, False) - (base + pl.program_id(0) * block)
    out_ref[...] = jnp.dot(
        onehot_lines(place, block), grads_ref[...], preferred_element_type=jnp.float32
    ).astype(out_ref.dtype)


def slot_sums(ids, grads, base, half, capacity):
    tokens, width = grads.shape
    block = min(512, half)
    return pl.pallas_call(
        functools.partial(sums_kernel, base=base, half=half, capacity=capacity),
        grid=(half // block,),
        in_specs=[
            pl.BlockSpec((1, tokens), lambda i: (0, 0)),
            pl.BlockSpec((tokens, width), lambda i: (0, 0)),
        ],
        out_specs=pl.BlockSpec((block, width), lambda i: (i, 0)),
        out_shape=jax.ShapeDtypeStruct((half, width), jnp.bfloat16),
        compiler_params=pltpu.CompilerParams(vmem_limit_bytes=16 * MIB),
        cost_estimate=pl.CostEstimate(
            flops=2 * half * tokens * width,
            bytes_accessed=2 * (tokens + half) * width,
            transcendentals=0,
        ),
        name="slot_sums",
    )(ids, grads)


def add_kernel(a_ref, b_ref, out_ref, lines, sems):
    chunks = sems.shape[0]
    piece = lines.shape[0] // chunks
    copies = []
    for chunk in range(chunks):
        at = slice(chunk * piece, (chunk + 1) * piece)
        total = a_ref[at, :].astype(jnp.float32) + b_ref[at, :].astype(jnp.float32)
        lines[at, :] = total.astype(jnp.bfloat16)
        window = pl.ds(chunk * piece, piece)
        copies.append(
            pltpu.make_async_copy(lines.at[window], out_ref.at[window], sems.at[chunk])
        )
        copies[-1].start()
    for copy in copies:
        copy.wait()


def add(a, b):
    vmem = pl.BlockSpec(memory_space=pltpu.VMEM)
    return pl.pallas_call(
        add_kernel,
        in_specs=[vmem] * 2,
        out_specs=pl.BlockSpec(memory_space=pl.ANY),
        out_shape=jax.ShapeDtypeStruct(a.shape, a.dtype),
        scratch_shapes=[pltpu.VMEM(a.shape, a.dtype), pltpu.SemaphoreType.DMA((4,))],
        compiler_params=pltpu.CompilerParams(vmem_limit_bytes=24 * MIB),
        cost_estimate=pl.CostEstimate(
            flops=a.size, bytes_accessed=6 * a.size, transcendentals=0
        ),
        name="add",
    )(a, b)


def prepare_kernel(
    rows_ref, emb_ref, acc_ref, ids_ref, old_ref, old_acc_ref, same_ref, cols_ref, *, half, capacity
):
    place = slot_place(ids_ref[...], capacity, half, True)
    for start in range(0, cols_ref.shape[0], 128):
        cols_ref[start : start + 128, :] = small(column(place[:, start : start + 128]))
    slots = rows_ref.shape[1]
    rows_dev = emb_ref.shape[0]
    rows = rows_ref[...]
    high = emb_ref[...].astype(jnp.bfloat16)
    low = (emb_ref[...] - high.astype(jnp.float32)).astype(jnp.bfloat16)
    row_lane = lax.broadcasted_iota(jnp.int32, (128, 128), 1)
    for start in range(0, slots, 128):
        at = slice(start, start + 128)
        col = column(rows[:, at])
        tiles = []
        acc = jnp.zeros((128, 128), jnp.float32)
        for tile in range(rows_dev // 128):
            hit = (row_lane + tile * 128) == col
            tiles.append(jnp.where(hit, 1.0, 0.0).astype(jnp.bfloat16))
            acc = acc + jnp.where(hit, acc_ref[tile : tile + 1, :], 0.0)
        onehot = jnp.concatenate(tiles, axis=1)
        old_ref[at, :] = jnp.dot(
            onehot, high, preferred_element_type=jnp.float32
        ) + jnp.dot(onehot, low, preferred_element_type=jnp.float32)
        acc = jnp.sum(acc, axis=1, keepdims=True)
        old_acc_ref[at, :] = jnp.where(col >= 0, acc, 1.0)
        for other in range(0, slots, 128):
            them = rows[:, other : other + 128]
            same_ref[at, other : other + 128] = jnp.where(
                (col == them) & (col >= 0), 1.0, 0.0
            ).astype(jnp.bfloat16)


def prepare(rows, embedding, row_accum, ids, half, capacity):
    rows_dev, width = embedding.shape
    slots = rows.shape[1]
    tokens = ids.shape[1]
    vmem = pl.BlockSpec(memory_space=pltpu.VMEM)
    return pl.pallas_call(
        functools.partial(prepare_kernel, half=half, capacity=capacity),
        in_specs=[vmem] * 4,
        out_specs=[vmem] * 4,
        out_shape=[
            jax.ShapeDtypeStruct((slots, width), jnp.float32),
            jax.ShapeDtypeStruct((slots, 128), jnp.float32),
            jax.ShapeDtypeStruct((slots, slots), jnp.bfloat16),
            jax.ShapeDtypeStruct((tokens, 128), jnp.int16),
        ],
        compiler_params=pltpu.CompilerParams(vmem_limit_bytes=24 * MIB),
        cost_estimate=pl.CostEstimate(
            flops=4 * rows_dev * slots * width,
            bytes_accessed=4 * rows_dev * width,
            transcendentals=0,
        ),
        name="prepare",
    )(rows, embedding, row_accum.reshape(rows_dev // 128, 128), ids)


def pick_kernel(arrived_ref, old_ref, acc_ref, same_ref, back_ref, sums_ref, lines, sems, *, places, back_places):
    capacity, width = arrived_ref.shape[1:]
    for host, members in enumerate(places):
        total = arrived_ref[members[0]].astype(jnp.float32)
        for place in members[1:]:
            total = total + arrived_ref[place].astype(jnp.float32)
        sums_ref[host * capacity : (host + 1) * capacity, :] = total.astype(jnp.bfloat16)
    grad = jnp.dot(same_ref[...], sums_ref[...], preferred_element_type=jnp.float32)
    square = jnp.mean(grad * grad, axis=1, keepdims=True)
    rate = 0.1 * lax.rsqrt(acc_ref[...] + square)
    for side in range(0, width, 128):
        lanes = slice(side, side + 128)
        new = (old_ref[:, lanes] - rate * grad[:, lanes]).astype(jnp.bfloat16)
        for host, members in enumerate(back_places):
            for place in members:
                lines[place, :, lanes] = new[host * capacity : (host + 1) * capacity]
    cut = lines.shape[0] // sems.shape[0]
    copies = []
    for part in range(sems.shape[0]):
        at = pl.ds(part * cut, cut)
        copies.append(pltpu.make_async_copy(lines.at[at], back_ref.at[at], sems.at[part]))
        copies[-1].start()
    for copy in copies:
        copy.wait()


def pick(arrived, old, old_acc, same, places, back_places):
    _, capacity, width = arrived.shape
    slots = len(places) * capacity
    vmem = pl.BlockSpec(memory_space=pltpu.VMEM)
    return pl.pallas_call(
        functools.partial(pick_kernel, places=places, back_places=back_places),
        in_specs=[vmem] * 4,
        out_specs=[pl.BlockSpec(memory_space=pl.ANY), vmem],
        out_shape=[
            jax.ShapeDtypeStruct(arrived.shape, jnp.bfloat16),
            jax.ShapeDtypeStruct((slots, width), jnp.bfloat16),
        ],
        scratch_shapes=[
            pltpu.VMEM(arrived.shape, jnp.bfloat16),
            pltpu.SemaphoreType.DMA((2,)),
        ],
        compiler_params=pltpu.CompilerParams(vmem_limit_bytes=24 * MIB),
        cost_estimate=pl.CostEstimate(
            flops=2 * slots * slots * width,
            bytes_accessed=8 * slots * width,
            transcendentals=slots,
        ),
        name="pick",
    )(arrived, old, old_acc, same)


def update_kernel(rows_ref, sums_ref, emb_ref, acc_ref, new_emb_ref, new_acc_ref):
    block, width = emb_ref.shape
    onehot = onehot_lines(rows_ref[...] - pl.program_id(0) * block, block)
    grad = jnp.dot(onehot, sums_ref[...], preferred_element_type=jnp.float32)
    square = jnp.mean(grad * grad, axis=1, keepdims=True)
    diagonal = lax.broadcasted_iota(jnp.int32, (128, 128), 0) == lax.broadcasted_iota(
        jnp.int32, (128, 128), 1
    )
    for part in range(block // 128):
        at = slice(part * 128, part * 128 + 128)
        acc = column(acc_ref[0, part : part + 1, :]) + square[at]
        new_acc_ref[0, part : part + 1, :] = jnp.sum(
            jnp.where(diagonal, acc, 0.0), axis=0, keepdims=True
        )
        rate = 0.1 * lax.rsqrt(acc)
        for side in range(0, width, 128):
            lanes = slice(side, side + 128)
            new_emb_ref[at, lanes] = emb_ref[at, lanes] - rate * grad[at, lanes]


def update(rows, sums, embedding, row_accum):
    rows_dev, width = embedding.shape
    slots = rows.shape[1]
    block = 512
    steps = rows_dev // block
    accum = row_accum.reshape(steps, block // 128, 128)
    table = pl.BlockSpec((block, width), lambda i: (i, 0))
    line = pl.BlockSpec((1, block // 128, 128), lambda i: (i, 0, 0))
    new_emb, new_acc = pl.pallas_call(
        update_kernel,
        grid=(steps,),
        in_specs=[
            pl.BlockSpec((1, slots), lambda i: (0, 0)),
            pl.BlockSpec((slots, width), lambda i: (0, 0)),
            table,
            line,
        ],
        out_specs=[table, line],
        out_shape=[
            jax.ShapeDtypeStruct((rows_dev, width), jnp.float32),
            jax.ShapeDtypeStruct(accum.shape, jnp.float32),
        ],
        compiler_params=pltpu.CompilerParams(vmem_limit_bytes=16 * MIB),
        cost_estimate=pl.CostEstimate(
            flops=2 * rows_dev * slots * width,
            bytes_accessed=8 * rows_dev * width,
            transcendentals=rows_dev,
        ),
        name="update",
    )(rows, sums, embedding, accum)
    return new_emb, new_acc.reshape(rows_dev)


def chosen_rows(cols, cache, base):
    slots = cache.shape[0]
    lane = lax.broadcasted_iota(jnp.int32, cols.shape, 1)
    onehot = jnp.concatenate(
        [matches(cols, small(lane + (base + start))) for start in range(0, slots, 128)], axis=1
    )
    return jnp.dot(onehot, cache, preferred_element_type=jnp.float32)


def first_expand_kernel(cols_ref, cache_ref, out_ref):
    block = min(1024, MIB // cache_ref.shape[0])
    for start in range(0, out_ref.shape[0], block):
        at = slice(start, start + block)
        out_ref[at, :] = chosen_rows(cols_ref[at, :], cache_ref[...], 0).astype(jnp.bfloat16)


def second_expand_kernel(cols_ref, cache_ref, before_ref, out_ref, lines, sems):
    block = lines.shape[0] // sems.shape[0]
    copies = []
    for start in range(0, lines.shape[0], block):
        at = slice(start, start + block)
        rows = chosen_rows(cols_ref[at, :], cache_ref[...], cache_ref.shape[0])
        lines[at, :] = (rows + before_ref[at, :].astype(jnp.float32)).astype(jnp.bfloat16)
        window = pl.ds(start, block)
        copies.append(
            pltpu.make_async_copy(lines.at[window], out_ref.at[window], sems.at[start // block])
        )
        copies[-1].start()
    for copy in copies:
        copy.wait()


def expand(cols, cache, before=None):
    slots, width = cache.shape
    tokens = cols.shape[0]
    vmem = pl.BlockSpec(memory_space=pltpu.VMEM)
    last = before is not None
    return pl.pallas_call(
        second_expand_kernel if last else first_expand_kernel,
        in_specs=[vmem] * (2 + last),
        out_specs=pl.BlockSpec(memory_space=pltpu.HBM) if last else vmem,
        out_shape=jax.ShapeDtypeStruct((tokens, width), jnp.bfloat16),
        scratch_shapes=[
            pltpu.VMEM((tokens, width), jnp.bfloat16),
            pltpu.SemaphoreType.DMA((tokens // 256,)),
        ]
        if last
        else [],
        compiler_params=pltpu.CompilerParams(vmem_limit_bytes=32 * MIB),
        cost_estimate=pl.CostEstimate(
            flops=2 * slots * tokens * width,
            bytes_accessed=2 * (tokens + slots) * width,
            transcendentals=0,
        ),
        name="second_expand" if last else "first_expand",
    )(cols, cache, *([before] if last else []))


def local(embedding, row_accum, lookup_grads, lookup_slot, owner_rows):
    n_hst = lax.axis_size("hst")
    chips = lax.axis_size("x")
    width = embedding.shape[1]
    capacity = owner_rows.shape[2]
    half = n_hst * chips * capacity

    def swap(block):
        return lax.ppermute(block, "core", [(0, 1), (1, 0)])

    members = n_hst * chips

    def places(back):
        order = chip_order(n_hst, chips, back)
        return [[order.index(h * chips + x) for x in range(chips)] for h in range(n_hst)]

    def exchange(blocks, back):
        order = chip_order(n_hst, chips, back)
        blocks = blocks.reshape(members, capacity, width)
        return lax.all_to_all(
            blocks, ("hst", "x"), split_axis=0, concat_axis=0, axis_index_groups=[order], tiled=True
        )

    rows = owner_rows.reshape(1, n_hst * capacity)
    ids = lookup_slot.reshape(1, -1)
    grads = load(lookup_grads)
    arrived = swap(slot_sums(ids, grads, half, half, capacity))
    kept = slot_sums(ids, grads, 0, half, capacity)
    arrived = exchange(add(kept, arrived), False)
    old, old_acc, same, cols = prepare(rows, embedding, row_accum, ids, half, capacity)
    back, sums = pick(arrived, old, old_acc, same, places(False), places(True))
    cache = exchange(back, True).reshape(half, width)
    new_embedding, new_accum = update(rows, sums, embedding, row_accum)
    cache, new_embedding, new_accum = lax.optimization_barrier((cache, new_embedding, new_accum))

    other = swap(cache)
    fresh_rows = expand(cols, cache)
    fresh_rows = expand(cols, other, fresh_rows)
    return (new_embedding, new_accum, fresh_rows)


def solution(mesh):
    chips = mesh.shape["local"] // 2
    fine = Mesh(mesh.devices.reshape(mesh.shape["hst"], chips, 2), ("hst", "x", "core"))
    whole = ("hst", "x", "core")
    return jax.shard_map(
        local,
        mesh=fine,
        in_specs=(P(whole, None), P(whole), P(whole, None), P(whole), P(whole, None, None)),
        out_specs=(P(whole, None), P(whole), P(whole, None)),
        check_vma=False,
    )
```

```python
import functools

import jax
import jax.numpy as jnp
from jax import lax
from jax.experimental import pallas as pl
from jax.experimental.pallas import tpu as pltpu
from jax.sharding import Mesh, PartitionSpec as P

MIB = 1024 * 1024


def bits_of(n):
    bits = n.bit_length() - 1
    assert n == 1 << bits
    return bits


def planes(n_hst):
    return 1 << (bits_of(n_hst) // 2)


def chip_order(n_hst, chips, back):
    n_y = planes(n_hst)
    n_z, n_yx = n_hst // n_y, n_y * chips
    mid = n_z // 2
    if back:
        zs = [*range(mid, n_z), *reversed(range(mid))]
        path = [z * n_yx + yx for z in zs for yx in reversed(range(n_yx))]
        first = n_yx // 2
        return path[first:] + path[:first]
    zs = [*reversed(range(mid + 1)), *reversed(range(mid + 1, n_z))]
    return [z * n_yx + (at ^ (n_yx // 2)) for at in range(n_yx) for z in zs]


def slot_place(ids, capacity, half, back):
    cap_bits = bits_of(capacity)
    other = ((ids >> cap_bits) & 1) ^ lax.axis_index("core")
    chip = ids >> (cap_bits + 1)
    place = jnp.zeros_like(chip)
    for at, member in enumerate(chip_order(lax.axis_size("hst"), lax.axis_size("x"), back)):
        place = jnp.where(chip == member, at, place)
    return other * half + (place << cap_bits) + (ids & (capacity - 1))


def column(row):
    return jnp.transpose(jnp.broadcast_to(row, (128, 128)))


def matches(a, b):
    return jnp.where(a == b, jnp.bfloat16(1), jnp.bfloat16(0))


def small(a):
    return a.astype(jnp.int16)


def onehot_lines(place, block):
    shape = (16, place.shape[1])
    slot = small(lax.broadcasted_iota(jnp.int32, shape, 0))
    place = small(jnp.broadcast_to(place, shape))
    return jnp.concatenate(
        [matches(slot, place - jnp.int16(start)) for start in range(0, block, 16)], axis=0
    )


def load_kernel(grads_ref, out_ref, sems):
    chunks = sems.shape[0]
    piece = out_ref.shape[0] // chunks
    copies = []
    for chunk in range(chunks):
        at = pl.ds(chunk * piece, piece)
        copies.append(pltpu.make_async_copy(grads_ref.at[at], out_ref.at[at], sems.at[chunk]))
        copies[-1].start()
    for copy in copies:
        copy.wait()


def load(grads):
    return pl.pallas_call(
        load_kernel,
        in_specs=[pl.BlockSpec(memory_space=pl.ANY)],
        out_specs=pl.BlockSpec(memory_space=pltpu.VMEM),
        out_shape=jax.ShapeDtypeStruct(grads.shape, grads.dtype),
        scratch_shapes=[pltpu.SemaphoreType.DMA((2,))],
        compiler_params=pltpu.CompilerParams(vmem_limit_bytes=52 * MIB),
        cost_estimate=pl.CostEstimate(
            flops=0, bytes_accessed=4 * grads.shape[0] * grads.shape[1], transcendentals=0
        ),
        name="load",
    )(grads)


def sums_kernel(ids_ref, grads_ref, out_ref, *, base, half, capacity):
    block = out_ref.shape[0]
    place = slot_place(ids_ref[...], capacity, half, False) - (base + pl.program_id(0) * block)
    out_ref[...] = jnp.dot(
        onehot_lines(place, block), grads_ref[...], preferred_element_type=jnp.float32
    ).astype(out_ref.dtype)


def slot_sums(ids, grads, base, half, capacity):
    tokens, width = grads.shape
    block = min(512, half)
    return pl.pallas_call(
        functools.partial(sums_kernel, base=base, half=half, capacity=capacity),
        grid=(half // block,),
        in_specs=[
            pl.BlockSpec((1, tokens), lambda i: (0, 0)),
            pl.BlockSpec((tokens, width), lambda i: (0, 0)),
        ],
        out_specs=pl.BlockSpec((block, width), lambda i: (i, 0)),
        out_shape=jax.ShapeDtypeStruct((half, width), jnp.bfloat16),
        compiler_params=pltpu.CompilerParams(vmem_limit_bytes=16 * MIB),
        cost_estimate=pl.CostEstimate(
            flops=2 * half * tokens * width,
            bytes_accessed=2 * (tokens + half) * width,
            transcendentals=0,
        ),
        name="slot_sums",
    )(ids, grads)


def add_kernel(a_ref, b_ref, out_ref, lines, sems):
    chunks = sems.shape[0]
    piece = lines.shape[0] // chunks
    copies = []
    for chunk in range(chunks):
        at = slice(chunk * piece, (chunk + 1) * piece)
        total = a_ref[at, :].astype(jnp.float32) + b_ref[at, :].astype(jnp.float32)
        lines[at, :] = total.astype(jnp.bfloat16)
        window = pl.ds(chunk * piece, piece)
        copies.append(
            pltpu.make_async_copy(lines.at[window], out_ref.at[window], sems.at[chunk])
        )
        copies[-1].start()
    for copy in copies:
        copy.wait()


def add(a, b):
    vmem = pl.BlockSpec(memory_space=pltpu.VMEM)
    return pl.pallas_call(
        add_kernel,
        in_specs=[vmem] * 2,
        out_specs=pl.BlockSpec(memory_space=pl.ANY),
        out_shape=jax.ShapeDtypeStruct(a.shape, a.dtype),
        scratch_shapes=[pltpu.VMEM(a.shape, a.dtype), pltpu.SemaphoreType.DMA((4,))],
        compiler_params=pltpu.CompilerParams(vmem_limit_bytes=24 * MIB),
        cost_estimate=pl.CostEstimate(
            flops=a.size, bytes_accessed=6 * a.size, transcendentals=0
        ),
        name="add",
    )(a, b)


def prepare_kernel(
    rows_ref, emb_ref, acc_ref, ids_ref, old_ref, old_acc_ref, same_ref, cols_ref, *, half, capacity
):
    place = slot_place(ids_ref[...], capacity, half, True)
    for start in range(0, cols_ref.shape[0], 128):
        cols_ref[start : start + 128, :] = small(column(place[:, start : start + 128]))
    slots = rows_ref.shape[1]
    rows_dev = emb_ref.shape[0]
    rows = rows_ref[...]
    high = emb_ref[...].astype(jnp.bfloat16)
    low = (emb_ref[...] - high.astype(jnp.float32)).astype(jnp.bfloat16)
    row_lane = lax.broadcasted_iota(jnp.int32, (128, 128), 1)
    for start in range(0, slots, 128):
        at = slice(start, start + 128)
        col = column(rows[:, at])
        tiles = []
        acc = jnp.zeros((128, 128), jnp.float32)
        for tile in range(rows_dev // 128):
            hit = (row_lane + tile * 128) == col
            tiles.append(jnp.where(hit, 1.0, 0.0).astype(jnp.bfloat16))
            acc = acc + jnp.where(hit, acc_ref[tile : tile + 1, :], 0.0)
        onehot = jnp.concatenate(tiles, axis=1)
        old_ref[at, :] = jnp.dot(
            onehot, high, preferred_element_type=jnp.float32
        ) + jnp.dot(onehot, low, preferred_element_type=jnp.float32)
        acc = jnp.sum(acc, axis=1, keepdims=True)
        old_acc_ref[at, :] = jnp.where(col >= 0, acc, 1.0)
        for other in range(0, slots, 128):
            them = rows[:, other : other + 128]
            same_ref[at, other : other + 128] = jnp.where(
                (col == them) & (col >= 0), 1.0, 0.0
            ).astype(jnp.bfloat16)


def prepare(rows, embedding, row_accum, ids, half, capacity):
    rows_dev, width = embedding.shape
    slots = rows.shape[1]
    tokens = ids.shape[1]
    vmem = pl.BlockSpec(memory_space=pltpu.VMEM)
    return pl.pallas_call(
        functools.partial(prepare_kernel, half=half, capacity=capacity),
        in_specs=[vmem] * 4,
        out_specs=[vmem] * 4,
        out_shape=[
            jax.ShapeDtypeStruct((slots, width), jnp.float32),
            jax.ShapeDtypeStruct((slots, 128), jnp.float32),
            jax.ShapeDtypeStruct((slots, slots), jnp.bfloat16),
            jax.ShapeDtypeStruct((tokens, 128), jnp.int16),
        ],
        compiler_params=pltpu.CompilerParams(vmem_limit_bytes=24 * MIB),
        cost_estimate=pl.CostEstimate(
            flops=4 * rows_dev * slots * width,
            bytes_accessed=4 * rows_dev * width,
            transcendentals=0,
        ),
        name="prepare",
    )(rows, embedding, row_accum.reshape(rows_dev // 128, 128), ids)


def pick_kernel(arrived_ref, old_ref, acc_ref, same_ref, back_ref, sums_ref, lines, sems, *, places, back_places):
    capacity, width = arrived_ref.shape[1:]
    for host, members in enumerate(places):
        total = arrived_ref[members[0]].astype(jnp.float32)
        for place in members[1:]:
            total = total + arrived_ref[place].astype(jnp.float32)
        sums_ref[host * capacity : (host + 1) * capacity, :] = total.astype(jnp.bfloat16)
    grad = jnp.dot(same_ref[...], sums_ref[...], preferred_element_type=jnp.float32)
    square = jnp.mean(grad * grad, axis=1, keepdims=True)
    rate = 0.1 * lax.rsqrt(acc_ref[...] + square)
    for side in range(0, width, 128):
        lanes = slice(side, side + 128)
        new = (old_ref[:, lanes] - rate * grad[:, lanes]).astype(jnp.bfloat16)
        for host, members in enumerate(back_places):
            for place in members:
                lines[place, :, lanes] = new[host * capacity : (host + 1) * capacity]
    cut = lines.shape[0] // sems.shape[0]
    copies = []
    for part in range(sems.shape[0]):
        at = pl.ds(part * cut, cut)
        copies.append(pltpu.make_async_copy(lines.at[at], back_ref.at[at], sems.at[part]))
        copies[-1].start()
    for copy in copies:
        copy.wait()


def pick(arrived, old, old_acc, same, places, back_places):
    _, capacity, width = arrived.shape
    slots = len(places) * capacity
    vmem = pl.BlockSpec(memory_space=pltpu.VMEM)
    return pl.pallas_call(
        functools.partial(pick_kernel, places=places, back_places=back_places),
        in_specs=[vmem] * 4,
        out_specs=[pl.BlockSpec(memory_space=pl.ANY), vmem],
        out_shape=[
            jax.ShapeDtypeStruct(arrived.shape, jnp.bfloat16),
            jax.ShapeDtypeStruct((slots, width), jnp.bfloat16),
        ],
        scratch_shapes=[
            pltpu.VMEM(arrived.shape, jnp.bfloat16),
            pltpu.SemaphoreType.DMA((2,)),
        ],
        compiler_params=pltpu.CompilerParams(vmem_limit_bytes=24 * MIB),
        cost_estimate=pl.CostEstimate(
            flops=2 * slots * slots * width,
            bytes_accessed=8 * slots * width,
            transcendentals=slots,
        ),
        name="pick",
    )(arrived, old, old_acc, same)


def update_kernel(rows_ref, sums_ref, emb_ref, acc_ref, new_emb_ref, new_acc_ref):
    block, width = emb_ref.shape
    onehot = onehot_lines(rows_ref[...] - pl.program_id(0) * block, block)
    grad = jnp.dot(onehot, sums_ref[...], preferred_element_type=jnp.float32)
    square = jnp.mean(grad * grad, axis=1, keepdims=True)
    diagonal = lax.broadcasted_iota(jnp.int32, (128, 128), 0) == lax.broadcasted_iota(
        jnp.int32, (128, 128), 1
    )
    for part in range(block // 128):
        at = slice(part * 128, part * 128 + 128)
        acc = column(acc_ref[0, part : part + 1, :]) + square[at]
        new_acc_ref[0, part : part + 1, :] = jnp.sum(
            jnp.where(diagonal, acc, 0.0), axis=0, keepdims=True
        )
        rate = 0.1 * lax.rsqrt(acc)
        for side in range(0, width, 128):
            lanes = slice(side, side + 128)
            new_emb_ref[at, lanes] = emb_ref[at, lanes] - rate * grad[at, lanes]


def update(rows, sums, embedding, row_accum):
    rows_dev, width = embedding.shape
    slots = rows.shape[1]
    block = 512
    steps = rows_dev // block
    accum = row_accum.reshape(steps, block // 128, 128)
    table = pl.BlockSpec((block, width), lambda i: (i, 0))
    line = pl.BlockSpec((1, block // 128, 128), lambda i: (i, 0, 0))
    new_emb, new_acc = pl.pallas_call(
        update_kernel,
        grid=(steps,),
        in_specs=[
            pl.BlockSpec((1, slots), lambda i: (0, 0)),
            pl.BlockSpec((slots, width), lambda i: (0, 0)),
            table,
            line,
        ],
        out_specs=[table, line],
        out_shape=[
            jax.ShapeDtypeStruct((rows_dev, width), jnp.float32),
            jax.ShapeDtypeStruct(accum.shape, jnp.float32),
        ],
        compiler_params=pltpu.CompilerParams(vmem_limit_bytes=16 * MIB),
        cost_estimate=pl.CostEstimate(
            flops=2 * rows_dev * slots * width,
            bytes_accessed=8 * rows_dev * width,
            transcendentals=rows_dev,
        ),
        name="update",
    )(rows, sums, embedding, accum)
    return new_emb, new_acc.reshape(rows_dev)


def chosen_rows(cols, cache, base):
    slots = cache.shape[0]
    lane = lax.broadcasted_iota(jnp.int32, cols.shape, 1)
    onehot = jnp.concatenate(
        [matches(cols, small(lane + (base + start))) for start in range(0, slots, 128)], axis=1
    )
    return jnp.dot(onehot, cache, preferred_element_type=jnp.float32)


def first_expand_kernel(cols_ref, cache_ref, out_ref):
    block = min(1024, MIB // cache_ref.shape[0])
    for start in range(0, out_ref.shape[0], block):
        at = slice(start, start + block)
        out_ref[at, :] = chosen_rows(cols_ref[at, :], cache_ref[...], 0).astype(jnp.bfloat16)


def second_expand_kernel(cols_ref, cache_ref, before_ref, out_ref, lines, sems):
    block = lines.shape[0] // sems.shape[0]
    copies = []
    for start in range(0, lines.shape[0], block):
        at = slice(start, start + block)
        rows = chosen_rows(cols_ref[at, :], cache_ref[...], cache_ref.shape[0])
        lines[at, :] = (rows + before_ref[at, :].astype(jnp.float32)).astype(jnp.bfloat16)
        window = pl.ds(start, block)
        copies.append(
            pltpu.make_async_copy(lines.at[window], out_ref.at[window], sems.at[start // block])
        )
        copies[-1].start()
    for copy in copies:
        copy.wait()


def expand(cols, cache, before=None):
    slots, width = cache.shape
    tokens = cols.shape[0]
    vmem = pl.BlockSpec(memory_space=pltpu.VMEM)
    last = before is not None
    return pl.pallas_call(
        second_expand_kernel if last else first_expand_kernel,
        in_specs=[vmem] * (2 + last),
        out_specs=pl.BlockSpec(memory_space=pltpu.HBM) if last else vmem,
        out_shape=jax.ShapeDtypeStruct((tokens, width), jnp.bfloat16),
        scratch_shapes=[
            pltpu.VMEM((tokens, width), jnp.bfloat16),
            pltpu.SemaphoreType.DMA((tokens // 256,)),
        ]
        if last
        else [],
        compiler_params=pltpu.CompilerParams(vmem_limit_bytes=32 * MIB),
        cost_estimate=pl.CostEstimate(
            flops=2 * slots * tokens * width,
            bytes_accessed=2 * (tokens + slots) * width,
            transcendentals=0,
        ),
        name="second_expand" if last else "first_expand",
    )(cols, cache, *([before] if last else []))


def local(embedding, row_accum, lookup_grads, lookup_slot, owner_rows):
    n_hst = lax.axis_size("hst")
    chips = lax.axis_size("x")
    width = embedding.shape[1]
    capacity = owner_rows.shape[2]
    half = n_hst * chips * capacity

    def swap(block):
        return lax.ppermute(block, "core", [(0, 1), (1, 0)])

    members = n_hst * chips

    def places(back):
        order = chip_order(n_hst, chips, back)
        return [[order.index(h * chips + x) for x in range(chips)] for h in range(n_hst)]

    def exchange(blocks, back):
        order = chip_order(n_hst, chips, back)
        blocks = blocks.reshape(members, capacity, width)
        return lax.all_to_all(
            blocks, ("hst", "x"), split_axis=0, concat_axis=0, axis_index_groups=[order], tiled=True
        )

    rows = owner_rows.reshape(1, n_hst * capacity)
    ids = lookup_slot.reshape(1, -1)
    grads = load(lookup_grads)
    arrived = swap(slot_sums(ids, grads, half, half, capacity))
    kept = slot_sums(ids, grads, 0, half, capacity)
    arrived = exchange(add(kept, arrived), False)
    old, old_acc, same, cols = prepare(rows, embedding, row_accum, ids, half, capacity)
    back, sums = pick(arrived, old, old_acc, same, places(False), places(True))
    cache = exchange(back, True).reshape(half, width)
    new_embedding, new_accum = update(rows, sums, embedding, row_accum)
    cache, new_embedding, new_accum = lax.optimization_barrier((cache, new_embedding, new_accum))

    other = swap(cache)
    fresh_rows = expand(cols, cache)
    fresh_rows = expand(cols, other, fresh_rows)
    return (new_embedding, new_accum, fresh_rows)


def solution(mesh):
    chips = mesh.shape["local"] // 2
    fine = Mesh(mesh.devices.reshape(mesh.shape["hst"], chips, 2), ("hst", "x", "core"))
    whole = ("hst", "x", "core")
    return jax.shard_map(
        local,
        mesh=fine,
        in_specs=(P(whole, None), P(whole), P(whole, None), P(whole), P(whole, None, None)),
        out_specs=(P(whole, None), P(whole), P(whole, None)),
        check_vma=False,
    )
```

```python
import functools

import jax
import jax.numpy as jnp
from jax import lax
from jax.experimental import pallas as pl
from jax.experimental.pallas import tpu as pltpu
from jax.sharding import Mesh, PartitionSpec as P

MIB = 1024 * 1024


def bits_of(n):
    bits = n.bit_length() - 1
    assert n == 1 << bits
    return bits


def planes(n_hst):
    return 1 << (bits_of(n_hst) // 2)


def chip_place(z, yx, n_z, n_yx, back):
    if back:
        return ((z + n_z // 2) & (n_z - 1)) * n_yx + (n_yx - 1 - yx)
    return (yx ^ (n_yx // 2)) * n_z + ((n_z // 2 - z) & (n_z - 1))


def member(host, chip, n_hst, chips, back):
    n_y = planes(n_hst)
    return chip_place(host // n_y, host % n_y * chips + chip, n_hst // n_y, n_y * chips, back)


def slot_place(ids, capacity, half, back):
    n_hst, chips = lax.axis_size("hst"), lax.axis_size("x")
    n_yx = planes(n_hst) * chips
    cap_bits = bits_of(capacity)
    other = ((ids >> cap_bits) & 1) ^ lax.axis_index("core")
    chip = ids >> (cap_bits + 1)
    place = chip_place(
        chip >> bits_of(n_yx), chip & (n_yx - 1), n_hst * chips // n_yx, n_yx, back
    )
    return other * half + (place << cap_bits) + (ids & (capacity - 1))


def column(row):
    return jnp.transpose(jnp.broadcast_to(row, (128, 128)))


def matches(a, b):
    return jnp.where(a == b, jnp.bfloat16(1), jnp.bfloat16(0))


def small(a):
    return a.astype(jnp.int16)


def onehot_lines(place, block):
    shape = (16, place.shape[1])
    slot = lax.broadcasted_iota(jnp.int32, (16, 128), 0)
    place = small(jnp.broadcast_to(place, shape))
    lines = []
    for start in range(0, block, 16):
        here = small(slot + start)
        lines.append(matches(jnp.concatenate([here] * (shape[1] // 128), axis=1), place))
    return jnp.concatenate(lines, axis=0)


def load_kernel(grads_ref, out_ref, sems):
    chunks = sems.shape[0]
    piece = out_ref.shape[0] // chunks
    copies = []
    for chunk in range(chunks):
        at = pl.ds(chunk * piece, piece)
        copies.append(pltpu.make_async_copy(grads_ref.at[at], out_ref.at[at], sems.at[chunk]))
        copies[-1].start()
    for copy in copies:
        copy.wait()


def load(grads):
    return pl.pallas_call(
        load_kernel,
        in_specs=[pl.BlockSpec(memory_space=pl.ANY)],
        out_specs=pl.BlockSpec(memory_space=pltpu.VMEM),
        out_shape=jax.ShapeDtypeStruct(grads.shape, grads.dtype),
        scratch_shapes=[pltpu.SemaphoreType.DMA((2,))],
        compiler_params=pltpu.CompilerParams(vmem_limit_bytes=52 * MIB),
        cost_estimate=pl.CostEstimate(
            flops=0, bytes_accessed=4 * grads.shape[0] * grads.shape[1], transcendentals=0
        ),
        name="load",
    )(grads)


def sums_kernel(ids_ref, grads_ref, out_ref, *, base, half, capacity):
    block = out_ref.shape[0]
    place = slot_place(ids_ref[...], capacity, half, False) - (base + pl.program_id(0) * block)
    out_ref[...] = jnp.dot(
        onehot_lines(place, block), grads_ref[...], preferred_element_type=jnp.float32
    ).astype(out_ref.dtype)


def slot_sums(ids, grads, base, half, capacity):
    tokens, width = grads.shape
    block = min(512, half)
    return pl.pallas_call(
        functools.partial(sums_kernel, base=base, half=half, capacity=capacity),
        grid=(half // block,),
        in_specs=[
            pl.BlockSpec((1, tokens), lambda i: (0, 0)),
            pl.BlockSpec((tokens, width), lambda i: (0, 0)),
        ],
        out_specs=pl.BlockSpec((block, width), lambda i: (i, 0)),
        out_shape=jax.ShapeDtypeStruct((half, width), jnp.bfloat16),
        compiler_params=pltpu.CompilerParams(vmem_limit_bytes=16 * MIB),
        cost_estimate=pl.CostEstimate(
            flops=2 * half * tokens * width,
            bytes_accessed=2 * (tokens + half) * width,
            transcendentals=0,
        ),
        name="slot_sums",
    )(ids, grads)


def add_kernel(a_ref, b_ref, out_ref, lines, sems):
    chunks = sems.shape[0]
    piece = lines.shape[0] // chunks
    copies = []
    for chunk in range(chunks):
        at = slice(chunk * piece, (chunk + 1) * piece)
        total = a_ref[at, :].astype(jnp.float32) + b_ref[at, :].astype(jnp.float32)
        lines[at, :] = total.astype(jnp.bfloat16)
        window = pl.ds(chunk * piece, piece)
        copies.append(
            pltpu.make_async_copy(lines.at[window], out_ref.at[window], sems.at[chunk])
        )
        copies[-1].start()
    for copy in copies:
        copy.wait()


def add(a, b):
    vmem = pl.BlockSpec(memory_space=pltpu.VMEM)
    return pl.pallas_call(
        add_kernel,
        in_specs=[vmem] * 2,
        out_specs=pl.BlockSpec(memory_space=pl.ANY),
        out_shape=jax.ShapeDtypeStruct(a.shape, a.dtype),
        scratch_shapes=[pltpu.VMEM(a.shape, a.dtype), pltpu.SemaphoreType.DMA((4,))],
        compiler_params=pltpu.CompilerParams(vmem_limit_bytes=24 * MIB),
        cost_estimate=pl.CostEstimate(
            flops=a.size, bytes_accessed=6 * a.size, transcendentals=0
        ),
        name="add",
    )(a, b)


def prepare_kernel(
    rows_ref, emb_ref, acc_ref, ids_ref, old_ref, old_acc_ref, same_ref, cols_ref, *, half, capacity
):
    place = slot_place(ids_ref[...], capacity, half, True)
    for start in range(0, cols_ref.shape[0], 128):
        cols_ref[start : start + 128, :] = small(column(place[:, start : start + 128]))
    slots = rows_ref.shape[1]
    rows_dev = emb_ref.shape[0]
    rows = rows_ref[...]
    high = emb_ref[...].astype(jnp.bfloat16)
    low = (emb_ref[...] - high.astype(jnp.float32)).astype(jnp.bfloat16)
    row_lane = lax.broadcasted_iota(jnp.int32, (128, 128), 1)
    for start in range(0, slots, 128):
        at = slice(start, start + 128)
        col = column(rows[:, at])
        tiles = []
        acc = jnp.zeros((128, 128), jnp.float32)
        for tile in range(rows_dev // 128):
            hit = (row_lane + tile * 128) == col
            tiles.append(jnp.where(hit, 1.0, 0.0).astype(jnp.bfloat16))
            acc = acc + jnp.where(hit, acc_ref[tile : tile + 1, :], 0.0)
        onehot = jnp.concatenate(tiles, axis=1)
        old_ref[at, :] = jnp.dot(
            onehot, high, preferred_element_type=jnp.float32
        ) + jnp.dot(onehot, low, preferred_element_type=jnp.float32)
        acc = jnp.sum(acc, axis=1, keepdims=True)
        old_acc_ref[at, :] = jnp.where(col >= 0, acc, 1.0)
        for other in range(0, slots, 128):
            them = rows[:, other : other + 128]
            same_ref[at, other : other + 128] = jnp.where(
                (col == them) & (col >= 0), 1.0, 0.0
            ).astype(jnp.bfloat16)


def prepare(rows, embedding, row_accum, ids, half, capacity):
    rows_dev, width = embedding.shape
    slots = rows.shape[1]
    tokens = ids.shape[1]
    vmem = pl.BlockSpec(memory_space=pltpu.VMEM)
    return pl.pallas_call(
        functools.partial(prepare_kernel, half=half, capacity=capacity),
        in_specs=[vmem] * 4,
        out_specs=[vmem] * 4,
        out_shape=[
            jax.ShapeDtypeStruct((slots, width), jnp.float32),
            jax.ShapeDtypeStruct((slots, 128), jnp.float32),
            jax.ShapeDtypeStruct((slots, slots), jnp.bfloat16),
            jax.ShapeDtypeStruct((tokens, 128), jnp.int16),
        ],
        compiler_params=pltpu.CompilerParams(vmem_limit_bytes=24 * MIB),
        cost_estimate=pl.CostEstimate(
            flops=4 * rows_dev * slots * width,
            bytes_accessed=4 * rows_dev * width,
            transcendentals=0,
        ),
        name="prepare",
    )(rows, embedding, row_accum.reshape(rows_dev // 128, 128), ids)


def pick_kernel(arrived_ref, old_ref, acc_ref, same_ref, back_ref, sums_ref, lines, sems, *, places, back_places):
    capacity, width = arrived_ref.shape[1:]
    for host, members in enumerate(places):
        total = arrived_ref[members[0]].astype(jnp.float32)
        for place in members[1:]:
            total = total + arrived_ref[place].astype(jnp.float32)
        sums_ref[host * capacity : (host + 1) * capacity, :] = total.astype(jnp.bfloat16)
    grad = jnp.dot(same_ref[...], sums_ref[...], preferred_element_type=jnp.float32)
    square = jnp.mean(grad * grad, axis=1, keepdims=True)
    rate = 0.1 * lax.rsqrt(acc_ref[...] + square)
    for side in range(0, width, 128):
        lanes = slice(side, side + 128)
        new = (old_ref[:, lanes] - rate * grad[:, lanes]).astype(jnp.bfloat16)
        for host, members in enumerate(back_places):
            for place in members:
                lines[place, :, lanes] = new[host * capacity : (host + 1) * capacity]
    cut = lines.shape[0] // sems.shape[0]
    copies = []
    for part in range(sems.shape[0]):
        at = pl.ds(part * cut, cut)
        copies.append(pltpu.make_async_copy(lines.at[at], back_ref.at[at], sems.at[part]))
        copies[-1].start()
    for copy in copies:
        copy.wait()


def pick(arrived, old, old_acc, same, places, back_places):
    _, capacity, width = arrived.shape
    slots = len(places) * capacity
    vmem = pl.BlockSpec(memory_space=pltpu.VMEM)
    return pl.pallas_call(
        functools.partial(pick_kernel, places=places, back_places=back_places),
        in_specs=[vmem] * 4,
        out_specs=[pl.BlockSpec(memory_space=pl.ANY), vmem],
        out_shape=[
            jax.ShapeDtypeStruct(arrived.shape, jnp.bfloat16),
            jax.ShapeDtypeStruct((slots, width), jnp.bfloat16),
        ],
        scratch_shapes=[
            pltpu.VMEM(arrived.shape, jnp.bfloat16),
            pltpu.SemaphoreType.DMA((2,)),
        ],
        compiler_params=pltpu.CompilerParams(vmem_limit_bytes=24 * MIB),
        cost_estimate=pl.CostEstimate(
            flops=2 * slots * slots * width,
            bytes_accessed=8 * slots * width,
            transcendentals=slots,
        ),
        name="pick",
    )(arrived, old, old_acc, same)


def update_kernel(rows_ref, sums_ref, emb_ref, acc_ref, new_emb_ref, new_acc_ref):
    block, width = emb_ref.shape
    onehot = onehot_lines(rows_ref[...] - pl.program_id(0) * block, block)
    grad = jnp.dot(onehot, sums_ref[...], preferred_element_type=jnp.float32)
    square = jnp.mean(grad * grad, axis=1, keepdims=True)
    diagonal = lax.broadcasted_iota(jnp.int32, (128, 128), 0) == lax.broadcasted_iota(
        jnp.int32, (128, 128), 1
    )
    for part in range(block // 128):
        at = slice(part * 128, part * 128 + 128)
        acc = column(acc_ref[0, part : part + 1, :]) + square[at]
        new_acc_ref[0, part : part + 1, :] = jnp.sum(
            jnp.where(diagonal, acc, 0.0), axis=0, keepdims=True
        )
        rate = 0.1 * lax.rsqrt(acc)
        for side in range(0, width, 128):
            lanes = slice(side, side + 128)
            new_emb_ref[at, lanes] = emb_ref[at, lanes] - rate * grad[at, lanes]


def update(rows, sums, embedding, row_accum):
    rows_dev, width = embedding.shape
    slots = rows.shape[1]
    block = 512
    steps = rows_dev // block
    accum = row_accum.reshape(steps, block // 128, 128)
    table = pl.BlockSpec((block, width), lambda i: (i, 0))
    line = pl.BlockSpec((1, block // 128, 128), lambda i: (i, 0, 0))
    new_emb, new_acc = pl.pallas_call(
        update_kernel,
        grid=(steps,),
        in_specs=[
            pl.BlockSpec((1, slots), lambda i: (0, 0)),
            pl.BlockSpec((slots, width), lambda i: (0, 0)),
            table,
            line,
        ],
        out_specs=[table, line],
        out_shape=[
            jax.ShapeDtypeStruct((rows_dev, width), jnp.float32),
            jax.ShapeDtypeStruct(accum.shape, jnp.float32),
        ],
        compiler_params=pltpu.CompilerParams(vmem_limit_bytes=16 * MIB),
        cost_estimate=pl.CostEstimate(
            flops=2 * rows_dev * slots * width,
            bytes_accessed=8 * rows_dev * width,
            transcendentals=rows_dev,
        ),
        name="update",
    )(rows, sums, embedding, accum)
    return new_emb, new_acc.reshape(rows_dev)


def chosen_rows(cols, cache, base):
    lookups = cols.shape[0]
    lane = lax.broadcasted_iota(jnp.int32, (16, 128), 1)
    tiles = []
    for start in range(0, cache.shape[0], 128):
        here = small(lane + (base + start))
        tiles.append(matches(cols, jnp.concatenate([here] * (lookups // 16), axis=0)))
    return jnp.dot(
        jnp.concatenate(tiles, axis=1), cache, preferred_element_type=jnp.float32
    ).astype(jnp.bfloat16)


def first_expand_kernel(cols_ref, cache_ref, out_ref):
    block = min(1024, MIB // cache_ref.shape[0])
    for start in range(0, out_ref.shape[0], block):
        at = slice(start, start + block)
        out_ref[at, :] = chosen_rows(cols_ref[at, :], cache_ref[...], 0)


def second_expand_kernel(cols_ref, cache_ref, before_ref, out_ref, lines, sems):
    block = lines.shape[0] // sems.shape[0]
    copies = []
    for start in range(0, lines.shape[0], block):
        at = slice(start, start + block)
        rows = chosen_rows(cols_ref[at, :], cache_ref[...], cache_ref.shape[0])
        lines[at, :] = rows + before_ref[at, :]
        window = pl.ds(start, block)
        copies.append(
            pltpu.make_async_copy(lines.at[window], out_ref.at[window], sems.at[start // block])
        )
        copies[-1].start()
    for copy in copies:
        copy.wait()


def expand(cols, cache, before=None):
    slots, width = cache.shape
    tokens = cols.shape[0]
    vmem = pl.BlockSpec(memory_space=pltpu.VMEM)
    last = before is not None
    return pl.pallas_call(
        second_expand_kernel if last else first_expand_kernel,
        in_specs=[vmem] * (2 + last),
        out_specs=pl.BlockSpec(memory_space=pltpu.HBM) if last else vmem,
        out_shape=jax.ShapeDtypeStruct((tokens, width), jnp.bfloat16),
        scratch_shapes=[
            pltpu.VMEM((tokens, width), jnp.bfloat16),
            pltpu.SemaphoreType.DMA((tokens // 256,)),
        ]
        if last
        else [],
        compiler_params=pltpu.CompilerParams(vmem_limit_bytes=32 * MIB),
        cost_estimate=pl.CostEstimate(
            flops=2 * slots * tokens * width,
            bytes_accessed=2 * (tokens + slots) * width,
            transcendentals=0,
        ),
        name="second_expand" if last else "first_expand",
    )(cols, cache, *([before] if last else []))


def local(embedding, row_accum, lookup_grads, lookup_slot, owner_rows):
    n_hst = lax.axis_size("hst")
    chips = lax.axis_size("x")
    width = embedding.shape[1]
    capacity = owner_rows.shape[2]
    half = n_hst * chips * capacity

    def swap(block):
        return lax.ppermute(block, "core", [(0, 1), (1, 0)])

    members = n_hst * chips

    def places(back):
        return [[member(h, x, n_hst, chips, back) for x in range(chips)] for h in range(n_hst)]

    def exchange(blocks, back):
        order = [0] * members
        for host, row in enumerate(places(back)):
            for chip, place in enumerate(row):
                order[place] = host * chips + chip
        blocks = blocks.reshape(members, capacity, width)
        return lax.all_to_all(
            blocks, ("hst", "x"), split_axis=0, concat_axis=0, axis_index_groups=[order], tiled=True
        )

    rows = owner_rows.reshape(1, n_hst * capacity)
    ids = lookup_slot.reshape(1, -1)
    grads = load(lookup_grads)
    arrived = swap(slot_sums(ids, grads, half, half, capacity))
    kept = slot_sums(ids, grads, 0, half, capacity)
    arrived = exchange(add(kept, arrived), False)
    old, old_acc, same, cols = prepare(rows, embedding, row_accum, ids, half, capacity)
    back, sums = pick(arrived, old, old_acc, same, places(False), places(True))
    cache = exchange(back, True).reshape(half, width)
    new_embedding, new_accum = update(rows, sums, embedding, row_accum)
    cache, new_embedding, new_accum = lax.optimization_barrier((cache, new_embedding, new_accum))

    other = swap(cache)
    fresh_rows = expand(cols, cache)
    fresh_rows = expand(cols, other, fresh_rows)
    return (new_embedding, new_accum, fresh_rows)


def solution(mesh):
    chips = mesh.shape["local"] // 2
    fine = Mesh(mesh.devices.reshape(mesh.shape["hst"], chips, 2), ("hst", "x", "core"))
    whole = ("hst", "x", "core")
    return jax.shard_map(
        local,
        mesh=fine,
        in_specs=(P(whole, None), P(whole), P(whole, None), P(whole), P(whole, None, None)),
        out_specs=(P(whole, None), P(whole), P(whole, None)),
        check_vma=False,
    )
```

```python
import functools

import jax
import jax.numpy as jnp
from jax import lax
from jax.experimental import pallas as pl
from jax.experimental.pallas import tpu as pltpu
from jax.sharding import Mesh, PartitionSpec as P

MIB = 1024 * 1024


def bits_of(n):
    bits = n.bit_length() - 1
    assert n == 1 << bits
    return bits


def planes(n_hst):
    return 1 << (bits_of(n_hst) // 2)


def chip_order(n_hst, chips, back):
    n_y = planes(n_hst)
    n_z, n_yx = n_hst // n_y, n_y * chips
    mid = n_z // 2
    if back:
        zs = [(mid + step) % n_z for step in range(n_z)]
        yxs = [*reversed(range(1, n_yx, 2)), *reversed(range(0, n_yx, 2))]
        return [z * n_yx + yx for z in zs for yx in yxs]
    zs = [(mid - step) % n_z for step in range(n_z)]
    yxs = [*range(n_yx // 2, n_yx), *reversed(range(n_yx // 2))]
    return [z * n_yx + yx for yx in yxs for z in zs]


def slot_place(ids, capacity, half, back):
    cap_bits = bits_of(capacity)
    other = ((ids >> cap_bits) & 1) ^ lax.axis_index("core")
    chip = ids >> (cap_bits + 1)
    place = jnp.zeros_like(chip)
    for at, member in enumerate(chip_order(lax.axis_size("hst"), lax.axis_size("x"), back)):
        place = jnp.where(chip == member, at, place)
    return other * half + (place << cap_bits) + (ids & (capacity - 1))


def column(row):
    return jnp.transpose(jnp.broadcast_to(row, (128, 128)))


def matches(a, b):
    return jnp.where(a == b, jnp.bfloat16(1), jnp.bfloat16(0))


def small(a):
    return a.astype(jnp.int16)


def onehot_lines(place, block):
    shape = (16, place.shape[1])
    slot = lax.broadcasted_iota(jnp.int32, (16, 128), 0)
    place = small(jnp.broadcast_to(place, shape))
    lines = []
    for start in range(0, block, 16):
        here = small(slot + start)
        lines.append(matches(jnp.concatenate([here] * (shape[1] // 128), axis=1), place))
    return jnp.concatenate(lines, axis=0)


def load_kernel(grads_ref, out_ref, sems):
    chunks = sems.shape[0]
    piece = out_ref.shape[0] // chunks
    copies = []
    for chunk in range(chunks):
        at = pl.ds(chunk * piece, piece)
        copies.append(pltpu.make_async_copy(grads_ref.at[at], out_ref.at[at], sems.at[chunk]))
        copies[-1].start()
    for copy in copies:
        copy.wait()


def load(grads):
    return pl.pallas_call(
        load_kernel,
        in_specs=[pl.BlockSpec(memory_space=pl.ANY)],
        out_specs=pl.BlockSpec(memory_space=pltpu.VMEM),
        out_shape=jax.ShapeDtypeStruct(grads.shape, grads.dtype),
        scratch_shapes=[pltpu.SemaphoreType.DMA((2,))],
        compiler_params=pltpu.CompilerParams(vmem_limit_bytes=52 * MIB),
        cost_estimate=pl.CostEstimate(
            flops=0, bytes_accessed=4 * grads.shape[0] * grads.shape[1], transcendentals=0
        ),
        name="load",
    )(grads)


def sums_kernel(ids_ref, grads_ref, out_ref, *, base, half, capacity):
    block = out_ref.shape[0]
    place = slot_place(ids_ref[...], capacity, half, False) - (base + pl.program_id(0) * block)
    out_ref[...] = jnp.dot(
        onehot_lines(place, block), grads_ref[...], preferred_element_type=jnp.float32
    ).astype(out_ref.dtype)


def slot_sums(ids, grads, base, half, capacity):
    tokens, width = grads.shape
    block = min(512, half)
    return pl.pallas_call(
        functools.partial(sums_kernel, base=base, half=half, capacity=capacity),
        grid=(half // block,),
        in_specs=[
            pl.BlockSpec((1, tokens), lambda i: (0, 0)),
            pl.BlockSpec((tokens, width), lambda i: (0, 0)),
        ],
        out_specs=pl.BlockSpec((block, width), lambda i: (i, 0)),
        out_shape=jax.ShapeDtypeStruct((half, width), jnp.bfloat16),
        compiler_params=pltpu.CompilerParams(vmem_limit_bytes=16 * MIB),
        cost_estimate=pl.CostEstimate(
            flops=2 * half * tokens * width,
            bytes_accessed=2 * (tokens + half) * width,
            transcendentals=0,
        ),
        name="slot_sums",
    )(ids, grads)


def add_kernel(a_ref, b_ref, out_ref, lines, sems):
    chunks = sems.shape[0]
    piece = lines.shape[0] // chunks
    copies = []
    for chunk in range(chunks):
        at = slice(chunk * piece, (chunk + 1) * piece)
        total = a_ref[at, :].astype(jnp.float32) + b_ref[at, :].astype(jnp.float32)
        lines[at, :] = total.astype(jnp.bfloat16)
        window = pl.ds(chunk * piece, piece)
        copies.append(
            pltpu.make_async_copy(lines.at[window], out_ref.at[window], sems.at[chunk])
        )
        copies[-1].start()
    for copy in copies:
        copy.wait()


def add(a, b):
    vmem = pl.BlockSpec(memory_space=pltpu.VMEM)
    return pl.pallas_call(
        add_kernel,
        in_specs=[vmem] * 2,
        out_specs=pl.BlockSpec(memory_space=pl.ANY),
        out_shape=jax.ShapeDtypeStruct(a.shape, a.dtype),
        scratch_shapes=[pltpu.VMEM(a.shape, a.dtype), pltpu.SemaphoreType.DMA((4,))],
        compiler_params=pltpu.CompilerParams(vmem_limit_bytes=24 * MIB),
        cost_estimate=pl.CostEstimate(
            flops=a.size, bytes_accessed=6 * a.size, transcendentals=0
        ),
        name="add",
    )(a, b)


def prepare_kernel(
    rows_ref, emb_ref, acc_ref, ids_ref, old_ref, old_acc_ref, same_ref, cols_ref, *, half, capacity
):
    place = slot_place(ids_ref[...], capacity, half, True)
    for start in range(0, cols_ref.shape[0], 128):
        cols_ref[start : start + 128, :] = small(column(place[:, start : start + 128]))
    slots = rows_ref.shape[1]
    rows_dev = emb_ref.shape[0]
    rows = rows_ref[...]
    high = emb_ref[...].astype(jnp.bfloat16)
    low = (emb_ref[...] - high.astype(jnp.float32)).astype(jnp.bfloat16)
    row_lane = lax.broadcasted_iota(jnp.int32, (128, 128), 1)
    for start in range(0, slots, 128):
        at = slice(start, start + 128)
        col = column(rows[:, at])
        tiles = []
        acc = jnp.zeros((128, 128), jnp.float32)
        for tile in range(rows_dev // 128):
            hit = (row_lane + tile * 128) == col
            tiles.append(jnp.where(hit, 1.0, 0.0).astype(jnp.bfloat16))
            acc = acc + jnp.where(hit, acc_ref[tile : tile + 1, :], 0.0)
        onehot = jnp.concatenate(tiles, axis=1)
        old_ref[at, :] = jnp.dot(
            onehot, high, preferred_element_type=jnp.float32
        ) + jnp.dot(onehot, low, preferred_element_type=jnp.float32)
        acc = jnp.sum(acc, axis=1, keepdims=True)
        old_acc_ref[at, :] = jnp.where(col >= 0, acc, 1.0)
        for other in range(0, slots, 128):
            them = rows[:, other : other + 128]
            same_ref[at, other : other + 128] = jnp.where(
                (col == them) & (col >= 0), 1.0, 0.0
            ).astype(jnp.bfloat16)


def prepare(rows, embedding, row_accum, ids, half, capacity):
    rows_dev, width = embedding.shape
    slots = rows.shape[1]
    tokens = ids.shape[1]
    vmem = pl.BlockSpec(memory_space=pltpu.VMEM)
    return pl.pallas_call(
        functools.partial(prepare_kernel, half=half, capacity=capacity),
        in_specs=[vmem] * 4,
        out_specs=[vmem] * 4,
        out_shape=[
            jax.ShapeDtypeStruct((slots, width), jnp.float32),
            jax.ShapeDtypeStruct((slots, 128), jnp.float32),
            jax.ShapeDtypeStruct((slots, slots), jnp.bfloat16),
            jax.ShapeDtypeStruct((tokens, 128), jnp.int16),
        ],
        compiler_params=pltpu.CompilerParams(vmem_limit_bytes=24 * MIB),
        cost_estimate=pl.CostEstimate(
            flops=4 * rows_dev * slots * width,
            bytes_accessed=4 * rows_dev * width,
            transcendentals=0,
        ),
        name="prepare",
    )(rows, embedding, row_accum.reshape(rows_dev // 128, 128), ids)


def pick_kernel(arrived_ref, old_ref, acc_ref, same_ref, back_ref, sums_ref, lines, sems, *, places, back_places):
    capacity, width = arrived_ref.shape[1:]
    for host, members in enumerate(places):
        total = arrived_ref[members[0]].astype(jnp.float32)
        for place in members[1:]:
            total = total + arrived_ref[place].astype(jnp.float32)
        sums_ref[host * capacity : (host + 1) * capacity, :] = total.astype(jnp.bfloat16)
    grad = jnp.dot(same_ref[...], sums_ref[...], preferred_element_type=jnp.float32)
    square = jnp.mean(grad * grad, axis=1, keepdims=True)
    rate = 0.1 * lax.rsqrt(acc_ref[...] + square)
    for side in range(0, width, 128):
        lanes = slice(side, side + 128)
        new = (old_ref[:, lanes] - rate * grad[:, lanes]).astype(jnp.bfloat16)
        for host, members in enumerate(back_places):
            for place in members:
                lines[place, :, lanes] = new[host * capacity : (host + 1) * capacity]
    cut = lines.shape[0] // sems.shape[0]
    copies = []
    for part in range(sems.shape[0]):
        at = pl.ds(part * cut, cut)
        copies.append(pltpu.make_async_copy(lines.at[at], back_ref.at[at], sems.at[part]))
        copies[-1].start()
    for copy in copies:
        copy.wait()


def pick(arrived, old, old_acc, same, places, back_places):
    _, capacity, width = arrived.shape
    slots = len(places) * capacity
    vmem = pl.BlockSpec(memory_space=pltpu.VMEM)
    return pl.pallas_call(
        functools.partial(pick_kernel, places=places, back_places=back_places),
        in_specs=[vmem] * 4,
        out_specs=[pl.BlockSpec(memory_space=pl.ANY), vmem],
        out_shape=[
            jax.ShapeDtypeStruct(arrived.shape, jnp.bfloat16),
            jax.ShapeDtypeStruct((slots, width), jnp.bfloat16),
        ],
        scratch_shapes=[
            pltpu.VMEM(arrived.shape, jnp.bfloat16),
            pltpu.SemaphoreType.DMA((2,)),
        ],
        compiler_params=pltpu.CompilerParams(vmem_limit_bytes=24 * MIB),
        cost_estimate=pl.CostEstimate(
            flops=2 * slots * slots * width,
            bytes_accessed=8 * slots * width,
            transcendentals=slots,
        ),
        name="pick",
    )(arrived, old, old_acc, same)


def update_kernel(rows_ref, sums_ref, emb_ref, acc_ref, new_emb_ref, new_acc_ref):
    block, width = emb_ref.shape
    onehot = onehot_lines(rows_ref[...] - pl.program_id(0) * block, block)
    grad = jnp.dot(onehot, sums_ref[...], preferred_element_type=jnp.float32)
    square = jnp.mean(grad * grad, axis=1, keepdims=True)
    diagonal = lax.broadcasted_iota(jnp.int32, (128, 128), 0) == lax.broadcasted_iota(
        jnp.int32, (128, 128), 1
    )
    for part in range(block // 128):
        at = slice(part * 128, part * 128 + 128)
        acc = column(acc_ref[0, part : part + 1, :]) + square[at]
        new_acc_ref[0, part : part + 1, :] = jnp.sum(
            jnp.where(diagonal, acc, 0.0), axis=0, keepdims=True
        )
        rate = 0.1 * lax.rsqrt(acc)
        for side in range(0, width, 128):
            lanes = slice(side, side + 128)
            new_emb_ref[at, lanes] = emb_ref[at, lanes] - rate * grad[at, lanes]


def update(rows, sums, embedding, row_accum):
    rows_dev, width = embedding.shape
    slots = rows.shape[1]
    block = 512
    steps = rows_dev // block
    accum = row_accum.reshape(steps, block // 128, 128)
    table = pl.BlockSpec((block, width), lambda i: (i, 0))
    line = pl.BlockSpec((1, block // 128, 128), lambda i: (i, 0, 0))
    new_emb, new_acc = pl.pallas_call(
        update_kernel,
        grid=(steps,),
        in_specs=[
            pl.BlockSpec((1, slots), lambda i: (0, 0)),
            pl.BlockSpec((slots, width), lambda i: (0, 0)),
            table,
            line,
        ],
        out_specs=[table, line],
        out_shape=[
            jax.ShapeDtypeStruct((rows_dev, width), jnp.float32),
            jax.ShapeDtypeStruct(accum.shape, jnp.float32),
        ],
        compiler_params=pltpu.CompilerParams(vmem_limit_bytes=16 * MIB),
        cost_estimate=pl.CostEstimate(
            flops=2 * rows_dev * slots * width,
            bytes_accessed=8 * rows_dev * width,
            transcendentals=rows_dev,
        ),
        name="update",
    )(rows, sums, embedding, accum)
    return new_emb, new_acc.reshape(rows_dev)


def chosen_rows(cols, cache, base):
    lookups = cols.shape[0]
    lane = lax.broadcasted_iota(jnp.int32, (16, 128), 1)
    tiles = []
    for start in range(0, cache.shape[0], 128):
        here = small(lane + (base + start))
        tiles.append(matches(cols, jnp.concatenate([here] * (lookups // 16), axis=0)))
    return jnp.dot(
        jnp.concatenate(tiles, axis=1), cache, preferred_element_type=jnp.float32
    ).astype(jnp.bfloat16)


def first_expand_kernel(cols_ref, cache_ref, out_ref):
    block = min(1024, MIB // cache_ref.shape[0])
    for start in range(0, out_ref.shape[0], block):
        at = slice(start, start + block)
        out_ref[at, :] = chosen_rows(cols_ref[at, :], cache_ref[...], 0)


def second_expand_kernel(cols_ref, cache_ref, before_ref, out_ref, lines, sems):
    block = lines.shape[0] // sems.shape[0]
    copies = []
    for start in range(0, lines.shape[0], block):
        at = slice(start, start + block)
        rows = chosen_rows(cols_ref[at, :], cache_ref[...], cache_ref.shape[0])
        lines[at, :] = rows + before_ref[at, :]
        window = pl.ds(start, block)
        copies.append(
            pltpu.make_async_copy(lines.at[window], out_ref.at[window], sems.at[start // block])
        )
        copies[-1].start()
    for copy in copies:
        copy.wait()


def expand(cols, cache, before=None):
    slots, width = cache.shape
    tokens = cols.shape[0]
    vmem = pl.BlockSpec(memory_space=pltpu.VMEM)
    last = before is not None
    return pl.pallas_call(
        second_expand_kernel if last else first_expand_kernel,
        in_specs=[vmem] * (2 + last),
        out_specs=pl.BlockSpec(memory_space=pltpu.HBM) if last else vmem,
        out_shape=jax.ShapeDtypeStruct((tokens, width), jnp.bfloat16),
        scratch_shapes=[
            pltpu.VMEM((tokens, width), jnp.bfloat16),
            pltpu.SemaphoreType.DMA((tokens // 256,)),
        ]
        if last
        else [],
        compiler_params=pltpu.CompilerParams(vmem_limit_bytes=32 * MIB),
        cost_estimate=pl.CostEstimate(
            flops=2 * slots * tokens * width,
            bytes_accessed=2 * (tokens + slots) * width,
            transcendentals=0,
        ),
        name="second_expand" if last else "first_expand",
    )(cols, cache, *([before] if last else []))


def local(embedding, row_accum, lookup_grads, lookup_slot, owner_rows):
    n_hst = lax.axis_size("hst")
    chips = lax.axis_size("x")
    width = embedding.shape[1]
    capacity = owner_rows.shape[2]
    half = n_hst * chips * capacity

    def swap(block):
        return lax.ppermute(block, "core", [(0, 1), (1, 0)])

    members = n_hst * chips

    def places(back):
        order = chip_order(n_hst, chips, back)
        return [[order.index(h * chips + x) for x in range(chips)] for h in range(n_hst)]

    def exchange(blocks, back):
        order = chip_order(n_hst, chips, back)
        blocks = blocks.reshape(members, capacity, width)
        return lax.all_to_all(
            blocks, ("hst", "x"), split_axis=0, concat_axis=0, axis_index_groups=[order], tiled=True
        )

    rows = owner_rows.reshape(1, n_hst * capacity)
    ids = lookup_slot.reshape(1, -1)
    grads = load(lookup_grads)
    arrived = swap(slot_sums(ids, grads, half, half, capacity))
    kept = slot_sums(ids, grads, 0, half, capacity)
    arrived = exchange(add(kept, arrived), False)
    old, old_acc, same, cols = prepare(rows, embedding, row_accum, ids, half, capacity)
    back, sums = pick(arrived, old, old_acc, same, places(False), places(True))
    cache = exchange(back, True).reshape(half, width)
    new_embedding, new_accum = update(rows, sums, embedding, row_accum)
    cache, new_embedding, new_accum = lax.optimization_barrier((cache, new_embedding, new_accum))

    other = swap(cache)
    fresh_rows = expand(cols, cache)
    fresh_rows = expand(cols, other, fresh_rows)
    return (new_embedding, new_accum, fresh_rows)


def solution(mesh):
    chips = mesh.shape["local"] // 2
    fine = Mesh(mesh.devices.reshape(mesh.shape["hst"], chips, 2), ("hst", "x", "core"))
    whole = ("hst", "x", "core")
    return jax.shard_map(
        local,
        mesh=fine,
        in_specs=(P(whole, None), P(whole), P(whole, None), P(whole), P(whole, None, None)),
        out_specs=(P(whole, None), P(whole), P(whole, None)),
        check_vma=False,
    )
```

```python
import functools

import jax
import jax.numpy as jnp
from jax import lax
from jax.experimental import pallas as pl
from jax.experimental.pallas import tpu as pltpu
from jax.sharding import Mesh, PartitionSpec as P

MIB = 1024 * 1024


def bits_of(n):
    bits = n.bit_length() - 1
    assert n == 1 << bits
    return bits


def planes(n_hst):
    return 1 << (bits_of(n_hst) // 2)


def chip_order(n_hst, chips, back, core):
    n_y = planes(n_hst)
    n_z, n_yx = n_hst // n_y, n_y * chips
    mid = n_z // 2
    flip = n_yx - 1 if core and not back else 0
    if back:
        zs = [(mid + step) % n_z for step in range(n_z)]
        yxs = [*reversed(range(1, n_yx, 2)), *reversed(range(0, n_yx, 2))]
        return [z * n_yx + (yx ^ flip) for z in zs for yx in yxs]
    zs = [(mid - step) % n_z for step in range(n_z)]
    yxs = [*range(n_yx // 2, n_yx), *reversed(range(n_yx // 2))]
    return [z * n_yx + (yx ^ flip) for yx in yxs for z in zs]


def slot_place(ids, capacity, half, back):
    cap_bits = bits_of(capacity)
    core = (ids >> cap_bits) & 1
    other = core ^ lax.axis_index("core")
    chip = ids >> (cap_bits + 1)
    place = jnp.zeros_like(chip)
    orders = [chip_order(lax.axis_size("hst"), lax.axis_size("x"), back, c) for c in range(2)]
    for member in range(len(orders[0])):
        at = jnp.where(core == 0, orders[0].index(member), orders[1].index(member))
        place = jnp.where(chip == member, at, place)
    return other * half + (place << cap_bits) + (ids & (capacity - 1))


def column(row):
    return jnp.transpose(jnp.broadcast_to(row, (128, 128)))


def matches(a, b):
    return jnp.where(a == b, jnp.bfloat16(1), jnp.bfloat16(0))


def small(a):
    return a.astype(jnp.int16)


def onehot_lines(place, block):
    shape = (16, place.shape[1])
    slot = lax.broadcasted_iota(jnp.int32, (16, 128), 0)
    place = small(jnp.broadcast_to(place, shape))
    lines = []
    for start in range(0, block, 16):
        here = small(slot + start)
        lines.append(matches(jnp.concatenate([here] * (shape[1] // 128), axis=1), place))
    return jnp.concatenate(lines, axis=0)


def load_kernel(grads_ref, out_ref, sems):
    chunks = sems.shape[0]
    piece = out_ref.shape[0] // chunks
    copies = []
    for chunk in range(chunks):
        at = pl.ds(chunk * piece, piece)
        copies.append(pltpu.make_async_copy(grads_ref.at[at], out_ref.at[at], sems.at[chunk]))
        copies[-1].start()
    for copy in copies:
        copy.wait()


def load(grads):
    return pl.pallas_call(
        load_kernel,
        in_specs=[pl.BlockSpec(memory_space=pl.ANY)],
        out_specs=pl.BlockSpec(memory_space=pltpu.VMEM),
        out_shape=jax.ShapeDtypeStruct(grads.shape, grads.dtype),
        scratch_shapes=[pltpu.SemaphoreType.DMA((2,))],
        compiler_params=pltpu.CompilerParams(vmem_limit_bytes=52 * MIB),
        cost_estimate=pl.CostEstimate(
            flops=0, bytes_accessed=4 * grads.shape[0] * grads.shape[1], transcendentals=0
        ),
        name="load",
    )(grads)


def sums_kernel(ids_ref, grads_ref, out_ref, *, base, half, capacity):
    block = out_ref.shape[0]
    place = slot_place(ids_ref[...], capacity, half, False) - (base + pl.program_id(0) * block)
    out_ref[...] = jnp.dot(
        onehot_lines(place, block), grads_ref[...], preferred_element_type=jnp.float32
    ).astype(out_ref.dtype)


def slot_sums(ids, grads, base, half, capacity):
    tokens, width = grads.shape
    block = min(512, half)
    return pl.pallas_call(
        functools.partial(sums_kernel, base=base, half=half, capacity=capacity),
        grid=(half // block,),
        in_specs=[
            pl.BlockSpec((1, tokens), lambda i: (0, 0)),
            pl.BlockSpec((tokens, width), lambda i: (0, 0)),
        ],
        out_specs=pl.BlockSpec((block, width), lambda i: (i, 0)),
        out_shape=jax.ShapeDtypeStruct((half, width), jnp.bfloat16),
        compiler_params=pltpu.CompilerParams(vmem_limit_bytes=16 * MIB),
        cost_estimate=pl.CostEstimate(
            flops=2 * half * tokens * width,
            bytes_accessed=2 * (tokens + half) * width,
            transcendentals=0,
        ),
        name="slot_sums",
    )(ids, grads)


def add_kernel(a_ref, b_ref, out_ref, lines, sems):
    chunks = sems.shape[0]
    piece = lines.shape[0] // chunks
    copies = []
    for chunk in range(chunks):
        at = slice(chunk * piece, (chunk + 1) * piece)
        total = a_ref[at, :].astype(jnp.float32) + b_ref[at, :].astype(jnp.float32)
        lines[at, :] = total.astype(jnp.bfloat16)
        window = pl.ds(chunk * piece, piece)
        copies.append(
            pltpu.make_async_copy(lines.at[window], out_ref.at[window], sems.at[chunk])
        )
        copies[-1].start()
    for copy in copies:
        copy.wait()


def add(a, b):
    vmem = pl.BlockSpec(memory_space=pltpu.VMEM)
    return pl.pallas_call(
        add_kernel,
        in_specs=[vmem] * 2,
        out_specs=pl.BlockSpec(memory_space=pl.ANY),
        out_shape=jax.ShapeDtypeStruct(a.shape, a.dtype),
        scratch_shapes=[pltpu.VMEM(a.shape, a.dtype), pltpu.SemaphoreType.DMA((4,))],
        compiler_params=pltpu.CompilerParams(vmem_limit_bytes=24 * MIB),
        cost_estimate=pl.CostEstimate(
            flops=a.size, bytes_accessed=6 * a.size, transcendentals=0
        ),
        name="add",
    )(a, b)


def prepare_kernel(
    rows_ref, emb_ref, acc_ref, ids_ref, old_ref, old_acc_ref, same_ref, cols_ref, *, half, capacity
):
    place = slot_place(ids_ref[...], capacity, half, True)
    for start in range(0, cols_ref.shape[0], 128):
        cols_ref[start : start + 128, :] = small(column(place[:, start : start + 128]))
    slots = rows_ref.shape[1]
    rows_dev = emb_ref.shape[0]
    rows = rows_ref[...]
    high = emb_ref[...].astype(jnp.bfloat16)
    low = (emb_ref[...] - high.astype(jnp.float32)).astype(jnp.bfloat16)
    row_lane = lax.broadcasted_iota(jnp.int32, (128, 128), 1)
    for start in range(0, slots, 128):
        at = slice(start, start + 128)
        col = column(rows[:, at])
        tiles = []
        acc = jnp.zeros((128, 128), jnp.float32)
        for tile in range(rows_dev // 128):
            hit = (row_lane + tile * 128) == col
            tiles.append(jnp.where(hit, 1.0, 0.0).astype(jnp.bfloat16))
            acc = acc + jnp.where(hit, acc_ref[tile : tile + 1, :], 0.0)
        onehot = jnp.concatenate(tiles, axis=1)
        old_ref[at, :] = jnp.dot(
            onehot, high, preferred_element_type=jnp.float32
        ) + jnp.dot(onehot, low, preferred_element_type=jnp.float32)
        acc = jnp.sum(acc, axis=1, keepdims=True)
        old_acc_ref[at, :] = jnp.where(col >= 0, acc, 1.0)
        for other in range(0, slots, 128):
            them = rows[:, other : other + 128]
            same_ref[at, other : other + 128] = jnp.where(
                (col == them) & (col >= 0), 1.0, 0.0
            ).astype(jnp.bfloat16)


def prepare(rows, embedding, row_accum, ids, half, capacity):
    rows_dev, width = embedding.shape
    slots = rows.shape[1]
    tokens = ids.shape[1]
    vmem = pl.BlockSpec(memory_space=pltpu.VMEM)
    return pl.pallas_call(
        functools.partial(prepare_kernel, half=half, capacity=capacity),
        in_specs=[vmem] * 4,
        out_specs=[vmem] * 4,
        out_shape=[
            jax.ShapeDtypeStruct((slots, width), jnp.float32),
            jax.ShapeDtypeStruct((slots, 128), jnp.float32),
            jax.ShapeDtypeStruct((slots, slots), jnp.bfloat16),
            jax.ShapeDtypeStruct((tokens, 128), jnp.int16),
        ],
        compiler_params=pltpu.CompilerParams(vmem_limit_bytes=24 * MIB),
        cost_estimate=pl.CostEstimate(
            flops=4 * rows_dev * slots * width,
            bytes_accessed=4 * rows_dev * width,
            transcendentals=0,
        ),
        name="prepare",
    )(rows, embedding, row_accum.reshape(rows_dev // 128, 128), ids)


def pick_kernel(*refs, places, back_places):
    for core in range(2):

        @pl.when(lax.axis_index("core") == core)
        def _():
            pick_rows(*refs, places[core], back_places[core])


def pick_rows(
    arrived_ref, old_ref, acc_ref, same_ref, back_ref, sums_ref, lines, sems, places, back_places
):
    capacity, width = arrived_ref.shape[1:]
    for host, members in enumerate(places):
        total = arrived_ref[members[0]].astype(jnp.float32)
        for place in members[1:]:
            total = total + arrived_ref[place].astype(jnp.float32)
        sums_ref[host * capacity : (host + 1) * capacity, :] = total.astype(jnp.bfloat16)
    grad = jnp.dot(same_ref[...], sums_ref[...], preferred_element_type=jnp.float32)
    square = jnp.mean(grad * grad, axis=1, keepdims=True)
    rate = 0.1 * lax.rsqrt(acc_ref[...] + square)
    for side in range(0, width, 128):
        lanes = slice(side, side + 128)
        new = (old_ref[:, lanes] - rate * grad[:, lanes]).astype(jnp.bfloat16)
        for host, members in enumerate(back_places):
            for place in members:
                lines[place, :, lanes] = new[host * capacity : (host + 1) * capacity]
    cut = lines.shape[0] // sems.shape[0]
    copies = []
    for part in range(sems.shape[0]):
        at = pl.ds(part * cut, cut)
        copies.append(pltpu.make_async_copy(lines.at[at], back_ref.at[at], sems.at[part]))
        copies[-1].start()
    for copy in copies:
        copy.wait()


def pick(arrived, old, old_acc, same, places, back_places):
    _, capacity, width = arrived.shape
    slots = len(places[0]) * capacity
    vmem = pl.BlockSpec(memory_space=pltpu.VMEM)
    return pl.pallas_call(
        functools.partial(pick_kernel, places=places, back_places=back_places),
        in_specs=[vmem] * 4,
        out_specs=[pl.BlockSpec(memory_space=pl.ANY), vmem],
        out_shape=[
            jax.ShapeDtypeStruct(arrived.shape, jnp.bfloat16),
            jax.ShapeDtypeStruct((slots, width), jnp.bfloat16),
        ],
        scratch_shapes=[
            pltpu.VMEM(arrived.shape, jnp.bfloat16),
            pltpu.SemaphoreType.DMA((2,)),
        ],
        compiler_params=pltpu.CompilerParams(vmem_limit_bytes=24 * MIB),
        cost_estimate=pl.CostEstimate(
            flops=2 * slots * slots * width,
            bytes_accessed=8 * slots * width,
            transcendentals=slots,
        ),
        name="pick",
    )(arrived, old, old_acc, same)


def update_kernel(rows_ref, sums_ref, emb_ref, acc_ref, new_emb_ref, new_acc_ref):
    block, width = emb_ref.shape
    onehot = onehot_lines(rows_ref[...] - pl.program_id(0) * block, block)
    grad = jnp.dot(onehot, sums_ref[...], preferred_element_type=jnp.float32)
    square = jnp.mean(grad * grad, axis=1, keepdims=True)
    diagonal = lax.broadcasted_iota(jnp.int32, (128, 128), 0) == lax.broadcasted_iota(
        jnp.int32, (128, 128), 1
    )
    for part in range(block // 128):
        at = slice(part * 128, part * 128 + 128)
        acc = column(acc_ref[0, part : part + 1, :]) + square[at]
        new_acc_ref[0, part : part + 1, :] = jnp.sum(
            jnp.where(diagonal, acc, 0.0), axis=0, keepdims=True
        )
        rate = 0.1 * lax.rsqrt(acc)
        for side in range(0, width, 128):
            lanes = slice(side, side + 128)
            new_emb_ref[at, lanes] = emb_ref[at, lanes] - rate * grad[at, lanes]


def update(rows, sums, embedding, row_accum):
    rows_dev, width = embedding.shape
    slots = rows.shape[1]
    block = 512
    steps = rows_dev // block
    accum = row_accum.reshape(steps, block // 128, 128)
    table = pl.BlockSpec((block, width), lambda i: (i, 0))
    line = pl.BlockSpec((1, block // 128, 128), lambda i: (i, 0, 0))
    new_emb, new_acc = pl.pallas_call(
        update_kernel,
        grid=(steps,),
        in_specs=[
            pl.BlockSpec((1, slots), lambda i: (0, 0)),
            pl.BlockSpec((slots, width), lambda i: (0, 0)),
            table,
            line,
        ],
        out_specs=[table, line],
        out_shape=[
            jax.ShapeDtypeStruct((rows_dev, width), jnp.float32),
            jax.ShapeDtypeStruct(accum.shape, jnp.float32),
        ],
        compiler_params=pltpu.CompilerParams(vmem_limit_bytes=16 * MIB),
        cost_estimate=pl.CostEstimate(
            flops=2 * rows_dev * slots * width,
            bytes_accessed=8 * rows_dev * width,
            transcendentals=rows_dev,
        ),
        name="update",
    )(rows, sums, embedding, accum)
    return new_emb, new_acc.reshape(rows_dev)


def chosen_rows(cols, cache, base):
    lookups = cols.shape[0]
    lane = lax.broadcasted_iota(jnp.int32, (16, 128), 1)
    tiles = []
    for start in range(0, cache.shape[0], 128):
        here = small(lane + (base + start))
        tiles.append(matches(cols, jnp.concatenate([here] * (lookups // 16), axis=0)))
    return jnp.dot(
        jnp.concatenate(tiles, axis=1), cache, preferred_element_type=jnp.float32
    ).astype(jnp.bfloat16)


def first_expand_kernel(cols_ref, cache_ref, out_ref):
    block = min(1024, MIB // cache_ref.shape[0])
    for start in range(0, out_ref.shape[0], block):
        at = slice(start, start + block)
        out_ref[at, :] = chosen_rows(cols_ref[at, :], cache_ref[...], 0)


def second_expand_kernel(cols_ref, cache_ref, before_ref, out_ref, lines, sems):
    block = lines.shape[0] // sems.shape[0]
    copies = []
    for start in range(0, lines.shape[0], block):
        at = slice(start, start + block)
        rows = chosen_rows(cols_ref[at, :], cache_ref[...], cache_ref.shape[0])
        lines[at, :] = rows + before_ref[at, :]
        window = pl.ds(start, block)
        copies.append(
            pltpu.make_async_copy(lines.at[window], out_ref.at[window], sems.at[start // block])
        )
        copies[-1].start()
    for copy in copies:
        copy.wait()


def expand(cols, cache, before=None):
    slots, width = cache.shape
    tokens = cols.shape[0]
    vmem = pl.BlockSpec(memory_space=pltpu.VMEM)
    last = before is not None
    return pl.pallas_call(
        second_expand_kernel if last else first_expand_kernel,
        in_specs=[vmem] * (2 + last),
        out_specs=pl.BlockSpec(memory_space=pltpu.HBM) if last else vmem,
        out_shape=jax.ShapeDtypeStruct((tokens, width), jnp.bfloat16),
        scratch_shapes=[
            pltpu.VMEM((tokens, width), jnp.bfloat16),
            pltpu.SemaphoreType.DMA((tokens // 256,)),
        ]
        if last
        else [],
        compiler_params=pltpu.CompilerParams(vmem_limit_bytes=32 * MIB),
        cost_estimate=pl.CostEstimate(
            flops=2 * slots * tokens * width,
            bytes_accessed=2 * (tokens + slots) * width,
            transcendentals=0,
        ),
        name="second_expand" if last else "first_expand",
    )(cols, cache, *([before] if last else []))


def local(embedding, row_accum, lookup_grads, lookup_slot, owner_rows):
    n_hst = lax.axis_size("hst")
    chips = lax.axis_size("x")
    width = embedding.shape[1]
    capacity = owner_rows.shape[2]
    half = n_hst * chips * capacity

    def swap(block):
        return lax.ppermute(block, "core", [(0, 1), (1, 0)])

    members = n_hst * chips

    def orders(back):
        return [chip_order(n_hst, chips, back, core) for core in range(2)]

    def places(back):
        return [
            [[order.index(h * chips + x) for x in range(chips)] for h in range(n_hst)]
            for order in orders(back)
        ]

    def exchange(blocks, back):
        groups = [[2 * chip + core for chip in order] for core, order in enumerate(orders(back))]
        blocks = blocks.reshape(members, capacity, width)
        return lax.all_to_all(
            blocks,
            ("hst", "x", "core"),
            split_axis=0,
            concat_axis=0,
            axis_index_groups=groups,
            tiled=True,
        )

    rows = owner_rows.reshape(1, n_hst * capacity)
    ids = lookup_slot.reshape(1, -1)
    grads = load(lookup_grads)
    arrived = swap(slot_sums(ids, grads, half, half, capacity))
    kept = slot_sums(ids, grads, 0, half, capacity)
    arrived = exchange(add(kept, arrived), False)
    old, old_acc, same, cols = prepare(rows, embedding, row_accum, ids, half, capacity)
    back, sums = pick(arrived, old, old_acc, same, places(False), places(True))
    cache = exchange(back, True).reshape(half, width)
    new_embedding, new_accum = update(rows, sums, embedding, row_accum)
    cache, new_embedding, new_accum = lax.optimization_barrier((cache, new_embedding, new_accum))

    other = swap(cache)
    fresh_rows = expand(cols, cache)
    fresh_rows = expand(cols, other, fresh_rows)
    return (new_embedding, new_accum, fresh_rows)


def solution(mesh):
    chips = mesh.shape["local"] // 2
    fine = Mesh(mesh.devices.reshape(mesh.shape["hst"], chips, 2), ("hst", "x", "core"))
    whole = ("hst", "x", "core")
    return jax.shard_map(
        local,
        mesh=fine,
        in_specs=(P(whole, None), P(whole), P(whole, None), P(whole), P(whole, None, None)),
        out_specs=(P(whole, None), P(whole), P(whole, None)),
        check_vma=False,
    )
```

```python
import functools

import jax
import jax.numpy as jnp
from jax import lax
from jax.experimental import pallas as pl
from jax.experimental.pallas import tpu as pltpu
from jax.sharding import Mesh, PartitionSpec as P

MIB = 1024 * 1024


def bits_of(n):
    bits = n.bit_length() - 1
    assert n == 1 << bits
    return bits


def planes(n_hst):
    return 1 << (bits_of(n_hst) // 2)


def chip_place(z, yx, n_z, n_yx, back):
    if back:
        return ((z + n_z // 2) & (n_z - 1)) * n_yx + (n_yx - 1 - yx)
    return (yx ^ (n_yx // 2)) * n_z + ((n_z // 2 - z) & (n_z - 1))


def member(host, chip, n_hst, chips, back):
    n_y = planes(n_hst)
    return chip_place(host // n_y, host % n_y * chips + chip, n_hst // n_y, n_y * chips, back)


def slot_place(ids, capacity, half, back):
    n_hst, chips = lax.axis_size("hst"), lax.axis_size("x")
    n_yx = planes(n_hst) * chips
    cap_bits = bits_of(capacity)
    other = ((ids >> cap_bits) & 1) ^ lax.axis_index("core")
    chip = ids >> (cap_bits + 1)
    place = chip_place(
        chip >> bits_of(n_yx), chip & (n_yx - 1), n_hst * chips // n_yx, n_yx, back
    )
    return other * half + (place << cap_bits) + (ids & (capacity - 1))


def column(row):
    return jnp.transpose(jnp.broadcast_to(row, (128, 128)))


def matches(a, b):
    return jnp.where(a == b, jnp.bfloat16(1), jnp.bfloat16(0))


def small(a):
    return a.astype(jnp.int16)


def onehot_lines(place, block):
    shape = (16, place.shape[1])
    slot = lax.broadcasted_iota(jnp.int32, (16, 128), 0)
    place = small(jnp.broadcast_to(place, shape))
    lines = []
    for start in range(0, block, 16):
        here = small(slot + start)
        lines.append(matches(jnp.concatenate([here] * (shape[1] // 128), axis=1), place))
    return jnp.concatenate(lines, axis=0)


def load_kernel(grads_ref, out_ref, sems):
    chunks = sems.shape[0]
    piece = out_ref.shape[0] // chunks
    copies = []
    for chunk in range(chunks):
        at = pl.ds(chunk * piece, piece)
        copies.append(pltpu.make_async_copy(grads_ref.at[at], out_ref.at[at], sems.at[chunk]))
        copies[-1].start()
    for copy in copies:
        copy.wait()


def load(grads):
    return pl.pallas_call(
        load_kernel,
        in_specs=[pl.BlockSpec(memory_space=pl.ANY)],
        out_specs=pl.BlockSpec(memory_space=pltpu.VMEM),
        out_shape=jax.ShapeDtypeStruct(grads.shape, grads.dtype),
        scratch_shapes=[pltpu.SemaphoreType.DMA((2,))],
        compiler_params=pltpu.CompilerParams(vmem_limit_bytes=52 * MIB),
        cost_estimate=pl.CostEstimate(
            flops=0, bytes_accessed=4 * grads.shape[0] * grads.shape[1], transcendentals=0
        ),
        name="load",
    )(grads)


def sums_kernel(ids_ref, grads_ref, out_ref, *, base, half, capacity):
    block = out_ref.shape[0]
    place = slot_place(ids_ref[...], capacity, half, False) - (base + pl.program_id(0) * block)
    out_ref[...] = jnp.dot(
        onehot_lines(place, block), grads_ref[...], preferred_element_type=jnp.float32
    ).astype(out_ref.dtype)


def slot_sums(ids, grads, base, half, capacity):
    tokens, width = grads.shape
    block = min(512, half)
    return pl.pallas_call(
        functools.partial(sums_kernel, base=base, half=half, capacity=capacity),
        grid=(half // block,),
        in_specs=[
            pl.BlockSpec((1, tokens), lambda i: (0, 0)),
            pl.BlockSpec((tokens, width), lambda i: (0, 0)),
        ],
        out_specs=pl.BlockSpec((block, width), lambda i: (i, 0)),
        out_shape=jax.ShapeDtypeStruct((half, width), jnp.bfloat16),
        compiler_params=pltpu.CompilerParams(vmem_limit_bytes=16 * MIB),
        cost_estimate=pl.CostEstimate(
            flops=2 * half * tokens * width,
            bytes_accessed=2 * (tokens + half) * width,
            transcendentals=0,
        ),
        name="slot_sums",
    )(ids, grads)


def add_kernel(a_ref, b_ref, out_ref, lines, sems):
    chunks = sems.shape[0]
    piece = lines.shape[0] // chunks
    copies = []
    for chunk in range(chunks):
        at = slice(chunk * piece, (chunk + 1) * piece)
        total = a_ref[at, :].astype(jnp.float32) + b_ref[at, :].astype(jnp.float32)
        lines[at, :] = total.astype(jnp.bfloat16)
        window = pl.ds(chunk * piece, piece)
        copies.append(
            pltpu.make_async_copy(lines.at[window], out_ref.at[window], sems.at[chunk])
        )
        copies[-1].start()
    for copy in copies:
        copy.wait()


def add(a, b):
    vmem = pl.BlockSpec(memory_space=pltpu.VMEM)
    return pl.pallas_call(
        add_kernel,
        in_specs=[vmem] * 2,
        out_specs=pl.BlockSpec(memory_space=pl.ANY),
        out_shape=jax.ShapeDtypeStruct(a.shape, a.dtype),
        scratch_shapes=[pltpu.VMEM(a.shape, a.dtype), pltpu.SemaphoreType.DMA((4,))],
        compiler_params=pltpu.CompilerParams(vmem_limit_bytes=24 * MIB),
        cost_estimate=pl.CostEstimate(
            flops=a.size, bytes_accessed=6 * a.size, transcendentals=0
        ),
        name="add",
    )(a, b)


def prepare_kernel(
    rows_ref, emb_ref, acc_ref, ids_ref, old_ref, old_acc_ref, same_ref, cols_ref, *, half, capacity
):
    place = slot_place(ids_ref[...], capacity, half, True)
    for start in range(0, cols_ref.shape[0], 128):
        cols_ref[start : start + 128, :] = small(column(place[:, start : start + 128]))
    slots = rows_ref.shape[1]
    rows_dev = emb_ref.shape[0]
    rows = rows_ref[...]
    high = emb_ref[...].astype(jnp.bfloat16)
    low = (emb_ref[...] - high.astype(jnp.float32)).astype(jnp.bfloat16)
    row_lane = lax.broadcasted_iota(jnp.int32, (128, 128), 1)
    for start in range(0, slots, 128):
        at = slice(start, start + 128)
        col = column(rows[:, at])
        tiles = []
        acc = jnp.zeros((128, 128), jnp.float32)
        for tile in range(rows_dev // 128):
            hit = (row_lane + tile * 128) == col
            tiles.append(jnp.where(hit, 1.0, 0.0).astype(jnp.bfloat16))
            acc = acc + jnp.where(hit, acc_ref[tile : tile + 1, :], 0.0)
        onehot = jnp.concatenate(tiles, axis=1)
        old_ref[at, :] = jnp.dot(
            onehot, high, preferred_element_type=jnp.float32
        ) + jnp.dot(onehot, low, preferred_element_type=jnp.float32)
        acc = jnp.sum(acc, axis=1, keepdims=True)
        old_acc_ref[at, :] = jnp.where(col >= 0, acc, 1.0)
        for other in range(0, slots, 128):
            them = rows[:, other : other + 128]
            same_ref[at, other : other + 128] = jnp.where(
                (col == them) & (col >= 0), 1.0, 0.0
            ).astype(jnp.bfloat16)


def prepare(rows, embedding, row_accum, ids, half, capacity):
    rows_dev, width = embedding.shape
    slots = rows.shape[1]
    tokens = ids.shape[1]
    vmem = pl.BlockSpec(memory_space=pltpu.VMEM)
    return pl.pallas_call(
        functools.partial(prepare_kernel, half=half, capacity=capacity),
        in_specs=[vmem] * 4,
        out_specs=[vmem] * 4,
        out_shape=[
            jax.ShapeDtypeStruct((slots, width), jnp.float32),
            jax.ShapeDtypeStruct((slots, 128), jnp.float32),
            jax.ShapeDtypeStruct((slots, slots), jnp.bfloat16),
            jax.ShapeDtypeStruct((tokens, 128), jnp.int16),
        ],
        compiler_params=pltpu.CompilerParams(vmem_limit_bytes=24 * MIB),
        cost_estimate=pl.CostEstimate(
            flops=4 * rows_dev * slots * width,
            bytes_accessed=4 * rows_dev * width,
            transcendentals=0,
        ),
        name="prepare",
    )(rows, embedding, row_accum.reshape(rows_dev // 128, 128), ids)


def pick_kernel(arrived_ref, old_ref, acc_ref, same_ref, back_ref, sums_ref, lines, sems, *, places, back_places):
    capacity, width = arrived_ref.shape[1:]
    for host, members in enumerate(places):
        total = arrived_ref[members[0]].astype(jnp.float32)
        for place in members[1:]:
            total = total + arrived_ref[place].astype(jnp.float32)
        sums_ref[host * capacity : (host + 1) * capacity, :] = total.astype(jnp.bfloat16)
    grad = jnp.dot(same_ref[...], sums_ref[...], preferred_element_type=jnp.float32)
    square = jnp.mean(grad * grad, axis=1, keepdims=True)
    rate = 0.1 * lax.rsqrt(acc_ref[...] + square)
    for side in range(0, width, 128):
        lanes = slice(side, side + 128)
        new = (old_ref[:, lanes] - rate * grad[:, lanes]).astype(jnp.bfloat16)
        for host, members in enumerate(back_places):
            for place in members:
                lines[place, :, lanes] = new[host * capacity : (host + 1) * capacity]
    cut = lines.shape[0] // sems.shape[0]
    copies = []
    for part in range(sems.shape[0]):
        at = pl.ds(part * cut, cut)
        copies.append(pltpu.make_async_copy(lines.at[at], back_ref.at[at], sems.at[part]))
        copies[-1].start()
    for copy in copies:
        copy.wait()


def pick(arrived, old, old_acc, same, places, back_places):
    _, capacity, width = arrived.shape
    slots = len(places) * capacity
    vmem = pl.BlockSpec(memory_space=pltpu.VMEM)
    return pl.pallas_call(
        functools.partial(pick_kernel, places=places, back_places=back_places),
        in_specs=[vmem] * 4,
        out_specs=[pl.BlockSpec(memory_space=pl.ANY), vmem],
        out_shape=[
            jax.ShapeDtypeStruct(arrived.shape, jnp.bfloat16),
            jax.ShapeDtypeStruct((slots, width), jnp.bfloat16),
        ],
        scratch_shapes=[
            pltpu.VMEM(arrived.shape, jnp.bfloat16),
            pltpu.SemaphoreType.DMA((2,)),
        ],
        compiler_params=pltpu.CompilerParams(vmem_limit_bytes=24 * MIB),
        cost_estimate=pl.CostEstimate(
            flops=2 * slots * slots * width,
            bytes_accessed=8 * slots * width,
            transcendentals=slots,
        ),
        name="pick",
    )(arrived, old, old_acc, same)


def update_kernel(rows_ref, sums_ref, emb_ref, acc_ref, new_emb_ref, new_acc_ref):
    block, width = emb_ref.shape
    onehot = onehot_lines(rows_ref[...] - pl.program_id(0) * block, block)
    grad = jnp.dot(onehot, sums_ref[...], preferred_element_type=jnp.float32)
    square = jnp.mean(grad * grad, axis=1, keepdims=True)
    diagonal = lax.broadcasted_iota(jnp.int32, (128, 128), 0) == lax.broadcasted_iota(
        jnp.int32, (128, 128), 1
    )
    for part in range(block // 128):
        at = slice(part * 128, part * 128 + 128)
        acc = column(acc_ref[0, part : part + 1, :]) + square[at]
        new_acc_ref[0, part : part + 1, :] = jnp.sum(
            jnp.where(diagonal, acc, 0.0), axis=0, keepdims=True
        )
        rate = 0.1 * lax.rsqrt(acc)
        for side in range(0, width, 128):
            lanes = slice(side, side + 128)
            new_emb_ref[at, lanes] = emb_ref[at, lanes] - rate * grad[at, lanes]


def update(rows, sums, embedding, row_accum):
    rows_dev, width = embedding.shape
    slots = rows.shape[1]
    block = 512
    steps = rows_dev // block
    accum = row_accum.reshape(steps, block // 128, 128)
    table = pl.BlockSpec((block, width), lambda i: (i, 0))
    line = pl.BlockSpec((1, block // 128, 128), lambda i: (i, 0, 0))
    new_emb, new_acc = pl.pallas_call(
        update_kernel,
        grid=(steps,),
        in_specs=[
            pl.BlockSpec((1, slots), lambda i: (0, 0)),
            pl.BlockSpec((slots, width), lambda i: (0, 0)),
            table,
            line,
        ],
        out_specs=[table, line],
        out_shape=[
            jax.ShapeDtypeStruct((rows_dev, width), jnp.float32),
            jax.ShapeDtypeStruct(accum.shape, jnp.float32),
        ],
        compiler_params=pltpu.CompilerParams(vmem_limit_bytes=16 * MIB),
        cost_estimate=pl.CostEstimate(
            flops=2 * rows_dev * slots * width,
            bytes_accessed=8 * rows_dev * width,
            transcendentals=rows_dev,
        ),
        name="update",
    )(rows, sums, embedding, accum)
    return new_emb, new_acc.reshape(rows_dev)


def chosen(cols, slots, base):
    lane = lax.broadcasted_iota(jnp.int32, (16, 128), 1)
    tiles = []
    for start in range(0, slots, 128):
        here = small(lane + (base + start))
        tiles.append(matches(cols, jnp.concatenate([here] * (cols.shape[0] // 16), axis=0)))
    return jnp.concatenate(tiles, axis=1)


def product(onehot, cache):
    return jnp.dot(onehot, cache, preferred_element_type=jnp.float32).astype(jnp.bfloat16)


def first_expand_kernel(cols_ref, cache_ref, out_ref, other_ref):
    slots = cache_ref.shape[0]
    block = min(1024, MIB // slots)
    for start in range(0, out_ref.shape[0], block):
        at = slice(start, start + block)
        out_ref[at, :] = product(chosen(cols_ref[at, :], slots, 0), cache_ref[...])
        other_ref[at, :] = chosen(cols_ref[at, :], slots, slots)


def first_expand(cols, cache):
    slots, width = cache.shape
    tokens = cols.shape[0]
    vmem = pl.BlockSpec(memory_space=pltpu.VMEM)
    return pl.pallas_call(
        first_expand_kernel,
        in_specs=[vmem] * 2,
        out_specs=[vmem] * 2,
        out_shape=[
            jax.ShapeDtypeStruct((tokens, width), jnp.bfloat16),
            jax.ShapeDtypeStruct((tokens, slots), jnp.bfloat16),
        ],
        compiler_params=pltpu.CompilerParams(vmem_limit_bytes=40 * MIB),
        cost_estimate=pl.CostEstimate(
            flops=2 * slots * tokens * width,
            bytes_accessed=2 * tokens * (width + slots),
            transcendentals=0,
        ),
        name="first_expand",
    )(cols, cache)


def second_expand_kernel(onehot_ref, cache_ref, before_ref, out_ref, lines, sems):
    block = lines.shape[0] // sems.shape[0]
    copies = []
    for start in range(0, lines.shape[0], block):
        at = slice(start, start + block)
        lines[at, :] = product(onehot_ref[at, :], cache_ref[...]) + before_ref[at, :]
        window = pl.ds(start, block)
        copies.append(
            pltpu.make_async_copy(lines.at[window], out_ref.at[window], sems.at[start // block])
        )
        copies[-1].start()
    for copy in copies:
        copy.wait()


def second_expand(onehot, cache, before):
    slots, width = cache.shape
    tokens = onehot.shape[0]
    vmem = pl.BlockSpec(memory_space=pltpu.VMEM)
    return pl.pallas_call(
        second_expand_kernel,
        in_specs=[vmem] * 3,
        out_specs=pl.BlockSpec(memory_space=pltpu.HBM),
        out_shape=jax.ShapeDtypeStruct((tokens, width), jnp.bfloat16),
        scratch_shapes=[
            pltpu.VMEM((tokens, width), jnp.bfloat16),
            pltpu.SemaphoreType.DMA((tokens // 256,)),
        ],
        compiler_params=pltpu.CompilerParams(vmem_limit_bytes=32 * MIB),
        cost_estimate=pl.CostEstimate(
            flops=2 * slots * tokens * width,
            bytes_accessed=2 * tokens * (width + slots),
            transcendentals=0,
        ),
        name="second_expand",
    )(onehot, cache, before)


def local(embedding, row_accum, lookup_grads, lookup_slot, owner_rows):
    n_hst = lax.axis_size("hst")
    chips = lax.axis_size("x")
    width = embedding.shape[1]
    capacity = owner_rows.shape[2]
    half = n_hst * chips * capacity

    def swap(block):
        return lax.ppermute(block, "core", [(0, 1), (1, 0)])

    members = n_hst * chips

    def places(back):
        return [[member(h, x, n_hst, chips, back) for x in range(chips)] for h in range(n_hst)]

    def exchange(blocks, back):
        order = [0] * members
        for host, row in enumerate(places(back)):
            for chip, place in enumerate(row):
                order[place] = host * chips + chip
        blocks = blocks.reshape(members, capacity, width)
        return lax.all_to_all(
            blocks, ("hst", "x"), split_axis=0, concat_axis=0, axis_index_groups=[order], tiled=True
        )

    rows = owner_rows.reshape(1, n_hst * capacity)
    ids = lookup_slot.reshape(1, -1)
    grads = load(lookup_grads)
    arrived = swap(slot_sums(ids, grads, half, half, capacity))
    kept = slot_sums(ids, grads, 0, half, capacity)
    arrived = exchange(add(kept, arrived), False)
    old, old_acc, same, cols = prepare(rows, embedding, row_accum, ids, half, capacity)
    back, sums = pick(arrived, old, old_acc, same, places(False), places(True))
    cache = exchange(back, True).reshape(half, width)
    new_embedding, new_accum = update(rows, sums, embedding, row_accum)
    cache, new_embedding, new_accum = lax.optimization_barrier((cache, new_embedding, new_accum))

    other = swap(cache)
    fresh_rows, onehot = first_expand(cols, cache)
    fresh_rows = second_expand(onehot, other, fresh_rows)
    return (new_embedding, new_accum, fresh_rows)


def solution(mesh):
    chips = mesh.shape["local"] // 2
    fine = Mesh(mesh.devices.reshape(mesh.shape["hst"], chips, 2), ("hst", "x", "core"))
    whole = ("hst", "x", "core")
    return jax.shard_map(
        local,
        mesh=fine,
        in_specs=(P(whole, None), P(whole), P(whole, None), P(whole), P(whole, None, None)),
        out_specs=(P(whole, None), P(whole), P(whole, None)),
        check_vma=False,
    )
```

```python
import functools

import jax
import jax.numpy as jnp
from jax import lax
from jax.experimental import pallas as pl
from jax.experimental.pallas import tpu as pltpu
from jax.sharding import Mesh, PartitionSpec as P

MIB = 1024 * 1024


def bits_of(n):
    bits = n.bit_length() - 1
    assert n == 1 << bits
    return bits


def planes(n_hst):
    return 1 << (bits_of(n_hst) // 2)


def chip_order(n_hst, chips, back):
    n_y = planes(n_hst)
    n_z, n_yx = n_hst // n_y, n_y * chips
    mid = n_z // 2
    if back:
        zs = [*range(mid, n_z), *reversed(range(mid))]
        yxs = [*reversed(range(1, n_yx, 2)), *reversed(range(0, n_yx, 2))]
        return [z * n_yx + yx for z in zs for yx in yxs]
    zs = [(mid - step) % n_z for step in range(n_z)]
    yxs = [*range(n_yx // 2, n_yx), *reversed(range(n_yx // 2))]
    return [z * n_yx + yx for yx in yxs for z in zs]


def slot_place(ids, capacity, half, back):
    cap_bits = bits_of(capacity)
    other = ((ids >> cap_bits) & 1) ^ lax.axis_index("core")
    chip = ids >> (cap_bits + 1)
    place = jnp.zeros_like(chip)
    for at, member in enumerate(chip_order(lax.axis_size("hst"), lax.axis_size("x"), back)):
        place = jnp.where(chip == member, at, place)
    return other * half + (place << cap_bits) + (ids & (capacity - 1))


def column(row):
    return jnp.transpose(jnp.broadcast_to(row, (128, 128)))


def matches(a, b):
    return jnp.where(a == b, jnp.bfloat16(1), jnp.bfloat16(0))


def small(a):
    return a.astype(jnp.int16)


def onehot_lines(place, block):
    shape = (16, place.shape[1])
    slot = lax.broadcasted_iota(jnp.int32, (16, 128), 0)
    place = small(jnp.broadcast_to(place, shape))
    lines = []
    for start in range(0, block, 16):
        here = small(slot + start)
        lines.append(matches(jnp.concatenate([here] * (shape[1] // 128), axis=1), place))
    return jnp.concatenate(lines, axis=0)


def load_kernel(grads_ref, out_ref, sems):
    chunks = sems.shape[0]
    piece = out_ref.shape[0] // chunks
    copies = []
    for chunk in range(chunks):
        at = pl.ds(chunk * piece, piece)
        copies.append(pltpu.make_async_copy(grads_ref.at[at], out_ref.at[at], sems.at[chunk]))
        copies[-1].start()
    for copy in copies:
        copy.wait()


def load(grads):
    return pl.pallas_call(
        load_kernel,
        in_specs=[pl.BlockSpec(memory_space=pl.ANY)],
        out_specs=pl.BlockSpec(memory_space=pltpu.VMEM),
        out_shape=jax.ShapeDtypeStruct(grads.shape, grads.dtype),
        scratch_shapes=[pltpu.SemaphoreType.DMA((2,))],
        compiler_params=pltpu.CompilerParams(vmem_limit_bytes=52 * MIB),
        cost_estimate=pl.CostEstimate(
            flops=0, bytes_accessed=4 * grads.shape[0] * grads.shape[1], transcendentals=0
        ),
        name="load",
    )(grads)


def sums_kernel(ids_ref, grads_ref, out_ref, *, base, half, capacity):
    block = out_ref.shape[0]
    place = slot_place(ids_ref[...], capacity, half, False) - (base + pl.program_id(0) * block)
    out_ref[...] = jnp.dot(
        onehot_lines(place, block), grads_ref[...], preferred_element_type=jnp.float32
    ).astype(out_ref.dtype)


def slot_sums(ids, grads, base, half, capacity):
    tokens, width = grads.shape
    block = min(512, half)
    return pl.pallas_call(
        functools.partial(sums_kernel, base=base, half=half, capacity=capacity),
        grid=(half // block,),
        in_specs=[
            pl.BlockSpec((1, tokens), lambda i: (0, 0)),
            pl.BlockSpec((tokens, width), lambda i: (0, 0)),
        ],
        out_specs=pl.BlockSpec((block, width), lambda i: (i, 0)),
        out_shape=jax.ShapeDtypeStruct((half, width), jnp.bfloat16),
        compiler_params=pltpu.CompilerParams(vmem_limit_bytes=16 * MIB),
        cost_estimate=pl.CostEstimate(
            flops=2 * half * tokens * width,
            bytes_accessed=2 * (tokens + half) * width,
            transcendentals=0,
        ),
        name="slot_sums",
    )(ids, grads)


def add_kernel(a_ref, b_ref, out_ref, lines, sems):
    chunks = sems.shape[0]
    piece = lines.shape[0] // chunks
    copies = []
    for chunk in range(chunks):
        at = slice(chunk * piece, (chunk + 1) * piece)
        total = a_ref[at, :].astype(jnp.float32) + b_ref[at, :].astype(jnp.float32)
        lines[at, :] = total.astype(jnp.bfloat16)
        window = pl.ds(chunk * piece, piece)
        copies.append(
            pltpu.make_async_copy(lines.at[window], out_ref.at[window], sems.at[chunk])
        )
        copies[-1].start()
    for copy in copies:
        copy.wait()


def add(a, b):
    vmem = pl.BlockSpec(memory_space=pltpu.VMEM)
    return pl.pallas_call(
        add_kernel,
        in_specs=[vmem] * 2,
        out_specs=pl.BlockSpec(memory_space=pl.ANY),
        out_shape=jax.ShapeDtypeStruct(a.shape, a.dtype),
        scratch_shapes=[pltpu.VMEM(a.shape, a.dtype), pltpu.SemaphoreType.DMA((4,))],
        compiler_params=pltpu.CompilerParams(vmem_limit_bytes=24 * MIB),
        cost_estimate=pl.CostEstimate(
            flops=a.size, bytes_accessed=6 * a.size, transcendentals=0
        ),
        name="add",
    )(a, b)


def prepare_kernel(
    rows_ref, emb_ref, acc_ref, ids_ref, old_ref, old_acc_ref, same_ref, cols_ref, *, half, capacity
):
    place = slot_place(ids_ref[...], capacity, half, True)
    for start in range(0, cols_ref.shape[0], 128):
        cols_ref[start : start + 128, :] = small(column(place[:, start : start + 128]))
    slots = rows_ref.shape[1]
    rows_dev = emb_ref.shape[0]
    rows = rows_ref[...]
    high = emb_ref[...].astype(jnp.bfloat16)
    low = (emb_ref[...] - high.astype(jnp.float32)).astype(jnp.bfloat16)
    row_lane = lax.broadcasted_iota(jnp.int32, (128, 128), 1)
    for start in range(0, slots, 128):
        at = slice(start, start + 128)
        col = column(rows[:, at])
        tiles = []
        acc = jnp.zeros((128, 128), jnp.float32)
        for tile in range(rows_dev // 128):
            hit = (row_lane + tile * 128) == col
            tiles.append(jnp.where(hit, 1.0, 0.0).astype(jnp.bfloat16))
            acc = acc + jnp.where(hit, acc_ref[tile : tile + 1, :], 0.0)
        onehot = jnp.concatenate(tiles, axis=1)
        old_ref[at, :] = jnp.dot(
            onehot, high, preferred_element_type=jnp.float32
        ) + jnp.dot(onehot, low, preferred_element_type=jnp.float32)
        acc = jnp.sum(acc, axis=1, keepdims=True)
        old_acc_ref[at, :] = jnp.where(col >= 0, acc, 1.0)
        for other in range(0, slots, 128):
            them = rows[:, other : other + 128]
            same_ref[at, other : other + 128] = jnp.where(
                (col == them) & (col >= 0), 1.0, 0.0
            ).astype(jnp.bfloat16)


def prepare(rows, embedding, row_accum, ids, half, capacity):
    rows_dev, width = embedding.shape
    slots = rows.shape[1]
    tokens = ids.shape[1]
    vmem = pl.BlockSpec(memory_space=pltpu.VMEM)
    return pl.pallas_call(
        functools.partial(prepare_kernel, half=half, capacity=capacity),
        in_specs=[vmem] * 4,
        out_specs=[vmem] * 4,
        out_shape=[
            jax.ShapeDtypeStruct((slots, width), jnp.float32),
            jax.ShapeDtypeStruct((slots, 128), jnp.float32),
            jax.ShapeDtypeStruct((slots, slots), jnp.bfloat16),
            jax.ShapeDtypeStruct((tokens, 128), jnp.int16),
        ],
        compiler_params=pltpu.CompilerParams(vmem_limit_bytes=24 * MIB),
        cost_estimate=pl.CostEstimate(
            flops=4 * rows_dev * slots * width,
            bytes_accessed=4 * rows_dev * width,
            transcendentals=0,
        ),
        name="prepare",
    )(rows, embedding, row_accum.reshape(rows_dev // 128, 128), ids)


def pick_kernel(arrived_ref, old_ref, acc_ref, same_ref, back_ref, sums_ref, lines, sems, *, places, back_places):
    capacity, width = arrived_ref.shape[1:]
    for host, members in enumerate(places):
        total = arrived_ref[members[0]].astype(jnp.float32)
        for place in members[1:]:
            total = total + arrived_ref[place].astype(jnp.float32)
        sums_ref[host * capacity : (host + 1) * capacity, :] = total.astype(jnp.bfloat16)
    grad = jnp.dot(same_ref[...], sums_ref[...], preferred_element_type=jnp.float32)
    square = jnp.mean(grad * grad, axis=1, keepdims=True)
    rate = 0.1 * lax.rsqrt(acc_ref[...] + square)
    for side in range(0, width, 128):
        lanes = slice(side, side + 128)
        new = (old_ref[:, lanes] - rate * grad[:, lanes]).astype(jnp.bfloat16)
        for host, members in enumerate(back_places):
            for place in members:
                lines[place, :, lanes] = new[host * capacity : (host + 1) * capacity]
    cut = lines.shape[0] // sems.shape[0]
    copies = []
    for part in range(sems.shape[0]):
        at = pl.ds(part * cut, cut)
        copies.append(pltpu.make_async_copy(lines.at[at], back_ref.at[at], sems.at[part]))
        copies[-1].start()
    for copy in copies:
        copy.wait()


def pick(arrived, old, old_acc, same, places, back_places):
    _, capacity, width = arrived.shape
    slots = len(places) * capacity
    vmem = pl.BlockSpec(memory_space=pltpu.VMEM)
    return pl.pallas_call(
        functools.partial(pick_kernel, places=places, back_places=back_places),
        in_specs=[vmem] * 4,
        out_specs=[pl.BlockSpec(memory_space=pl.ANY), vmem],
        out_shape=[
            jax.ShapeDtypeStruct(arrived.shape, jnp.bfloat16),
            jax.ShapeDtypeStruct((slots, width), jnp.bfloat16),
        ],
        scratch_shapes=[
            pltpu.VMEM(arrived.shape, jnp.bfloat16),
            pltpu.SemaphoreType.DMA((2,)),
        ],
        compiler_params=pltpu.CompilerParams(vmem_limit_bytes=24 * MIB),
        cost_estimate=pl.CostEstimate(
            flops=2 * slots * slots * width,
            bytes_accessed=8 * slots * width,
            transcendentals=slots,
        ),
        name="pick",
    )(arrived, old, old_acc, same)


def update_kernel(rows_ref, sums_ref, emb_ref, acc_ref, new_emb_ref, new_acc_ref):
    block, width = emb_ref.shape
    onehot = onehot_lines(rows_ref[...] - pl.program_id(0) * block, block)
    grad = jnp.dot(onehot, sums_ref[...], preferred_element_type=jnp.float32)
    square = jnp.mean(grad * grad, axis=1, keepdims=True)
    diagonal = lax.broadcasted_iota(jnp.int32, (128, 128), 0) == lax.broadcasted_iota(
        jnp.int32, (128, 128), 1
    )
    for part in range(block // 128):
        at = slice(part * 128, part * 128 + 128)
        acc = column(acc_ref[0, part : part + 1, :]) + square[at]
        new_acc_ref[0, part : part + 1, :] = jnp.sum(
            jnp.where(diagonal, acc, 0.0), axis=0, keepdims=True
        )
        rate = 0.1 * lax.rsqrt(acc)
        for side in range(0, width, 128):
            lanes = slice(side, side + 128)
            new_emb_ref[at, lanes] = emb_ref[at, lanes] - rate * grad[at, lanes]


def update(rows, sums, embedding, row_accum):
    rows_dev, width = embedding.shape
    slots = rows.shape[1]
    block = 512
    steps = rows_dev // block
    accum = row_accum.reshape(steps, block // 128, 128)
    table = pl.BlockSpec((block, width), lambda i: (i, 0))
    line = pl.BlockSpec((1, block // 128, 128), lambda i: (i, 0, 0))
    new_emb, new_acc = pl.pallas_call(
        update_kernel,
        grid=(steps,),
        in_specs=[
            pl.BlockSpec((1, slots), lambda i: (0, 0)),
            pl.BlockSpec((slots, width), lambda i: (0, 0)),
            table,
            line,
        ],
        out_specs=[table, line],
        out_shape=[
            jax.ShapeDtypeStruct((rows_dev, width), jnp.float32),
            jax.ShapeDtypeStruct(accum.shape, jnp.float32),
        ],
        compiler_params=pltpu.CompilerParams(vmem_limit_bytes=16 * MIB),
        cost_estimate=pl.CostEstimate(
            flops=2 * rows_dev * slots * width,
            bytes_accessed=8 * rows_dev * width,
            transcendentals=rows_dev,
        ),
        name="update",
    )(rows, sums, embedding, accum)
    return new_emb, new_acc.reshape(rows_dev)


def chosen_rows(cols, cache, base):
    lookups = cols.shape[0]
    lane = lax.broadcasted_iota(jnp.int32, (16, 128), 1)
    tiles = []
    for start in range(0, cache.shape[0], 128):
        here = small(lane + (base + start))
        tiles.append(matches(cols, jnp.concatenate([here] * (lookups // 16), axis=0)))
    return jnp.dot(
        jnp.concatenate(tiles, axis=1), cache, preferred_element_type=jnp.float32
    ).astype(jnp.bfloat16)


def first_expand_kernel(cols_ref, cache_ref, out_ref):
    block = min(1024, MIB // cache_ref.shape[0])
    for start in range(0, out_ref.shape[0], block):
        at = slice(start, start + block)
        out_ref[at, :] = chosen_rows(cols_ref[at, :], cache_ref[...], 0)


def second_expand_kernel(cols_ref, cache_ref, before_ref, out_ref, lines, sems):
    block = lines.shape[0] // sems.shape[0]
    copies = []
    for start in range(0, lines.shape[0], block):
        at = slice(start, start + block)
        rows = chosen_rows(cols_ref[at, :], cache_ref[...], cache_ref.shape[0])
        lines[at, :] = rows + before_ref[at, :]
        window = pl.ds(start, block)
        copies.append(
            pltpu.make_async_copy(lines.at[window], out_ref.at[window], sems.at[start // block])
        )
        copies[-1].start()
    for copy in copies:
        copy.wait()


def expand(cols, cache, before=None):
    slots, width = cache.shape
    tokens = cols.shape[0]
    vmem = pl.BlockSpec(memory_space=pltpu.VMEM)
    last = before is not None
    return pl.pallas_call(
        second_expand_kernel if last else first_expand_kernel,
        in_specs=[vmem] * (2 + last),
        out_specs=pl.BlockSpec(memory_space=pltpu.HBM) if last else vmem,
        out_shape=jax.ShapeDtypeStruct((tokens, width), jnp.bfloat16),
        scratch_shapes=[
            pltpu.VMEM((tokens, width), jnp.bfloat16),
            pltpu.SemaphoreType.DMA((tokens // 256,)),
        ]
        if last
        else [],
        compiler_params=pltpu.CompilerParams(vmem_limit_bytes=32 * MIB),
        cost_estimate=pl.CostEstimate(
            flops=2 * slots * tokens * width,
            bytes_accessed=2 * (tokens + slots) * width,
            transcendentals=0,
        ),
        name="second_expand" if last else "first_expand",
    )(cols, cache, *([before] if last else []))


def local(embedding, row_accum, lookup_grads, lookup_slot, owner_rows):
    n_hst = lax.axis_size("hst")
    chips = lax.axis_size("x")
    width = embedding.shape[1]
    capacity = owner_rows.shape[2]
    half = n_hst * chips * capacity

    def swap(block):
        return lax.ppermute(block, "core", [(0, 1), (1, 0)])

    members = n_hst * chips

    def places(back):
        order = chip_order(n_hst, chips, back)
        return [[order.index(h * chips + x) for x in range(chips)] for h in range(n_hst)]

    def exchange(blocks, back):
        order = chip_order(n_hst, chips, back)
        blocks = blocks.reshape(members, capacity, width)
        return lax.all_to_all(
            blocks, ("hst", "x"), split_axis=0, concat_axis=0, axis_index_groups=[order], tiled=True
        )

    rows = owner_rows.reshape(1, n_hst * capacity)
    ids = lookup_slot.reshape(1, -1)
    grads = load(lookup_grads)
    arrived = swap(slot_sums(ids, grads, half, half, capacity))
    kept = slot_sums(ids, grads, 0, half, capacity)
    arrived = exchange(add(kept, arrived), False)
    old, old_acc, same, cols = prepare(rows, embedding, row_accum, ids, half, capacity)
    back, sums = pick(arrived, old, old_acc, same, places(False), places(True))
    cache = exchange(back, True).reshape(half, width)
    new_embedding, new_accum = update(rows, sums, embedding, row_accum)
    cache, new_embedding, new_accum = lax.optimization_barrier((cache, new_embedding, new_accum))

    other = swap(cache)
    fresh_rows = expand(cols, cache)
    fresh_rows = expand(cols, other, fresh_rows)
    return (new_embedding, new_accum, fresh_rows)


def solution(mesh):
    chips = mesh.shape["local"] // 2
    fine = Mesh(mesh.devices.reshape(mesh.shape["hst"], chips, 2), ("hst", "x", "core"))
    whole = ("hst", "x", "core")
    return jax.shard_map(
        local,
        mesh=fine,
        in_specs=(P(whole, None), P(whole), P(whole, None), P(whole), P(whole, None, None)),
        out_specs=(P(whole, None), P(whole), P(whole, None)),
        check_vma=False,
    )
```
